32 devices in a mesh: feat: 4 (over x, core), samp: 8 (over z, y).
Axes of the slice: x: 2, y: 2, z: 4, core: 2. Of those that a mesh axis runs over, the one named last changes fastest.
Arguments:
- tier_one: bfloat16 [8192, 3072], P('feat', 'samp')
- residuals: bfloat16 [3072, 128], P('samp'), may hold values from -6 to 6
- pair_list: int32 [3, 16384], P(None, 'feat'), may hold values from 0 to 8191, as said below
Outputs:
- scores: float32 [16384, 128], P(('feat', 'samp'))
The draws below stay inside these ranges and needn't reach their ends.
Inputs may be any that keep to these rules, and one draw needn't show every extreme that they name: `pair_list`: rows 0 and 1 are feature indices, row 2 an operator id of 0 to 3; each descriptor's two features differ.
All inputs are finite; a program needn't handle non-finite values.
Results may differ from the reference program's by a relative error of at most 0.0031.
Values may be sent and summed in bfloat16 or wider, within the bound.
A program may use at most 64 MiB of HBM per device.

```python
import math
import jax
import jax.numpy as jnp
from jax import lax

F1 = 8192
K = 128
P_SIZE = 16384
SAMPLES = 3072


def draw_tier_one(key, part):
    keys = jax.random.split(key, 4)
    sample_pos = jnp.arange(SAMPLES, dtype=jnp.float32)
    rising = 1.0 + 2.0 * sample_pos / max(SAMPLES - 1, 1)
    feat_scale = jnp.exp(jax.random.uniform(keys[0], (F1, 1), jnp.float32, math.log(0.3), math.log(3.0)))
    feat_mean = jax.random.uniform(keys[1], (F1, 1), jnp.float32, -1.0, 1.0)
    roughness = jnp.exp(jax.random.uniform(keys[2], (1, SAMPLES), jnp.float32, math.log(0.5), math.log(2.0)))
    noise_part = jnp.clip(jax.random.normal(keys[3], (F1, SAMPLES), jnp.float32), -4.0, 4.0)
    return (feat_mean + feat_scale * rising[None, :] * roughness * noise_part).astype(jnp.bfloat16)


def draw_pair_list(key, part):
    keys = jax.random.split(jax.random.fold_in(key, 7), 3)
    first_idx = jax.random.randint(keys[0], (P_SIZE,), 0, F1, jnp.int32)
    offset = jax.random.randint(keys[1], (P_SIZE,), 1, F1, jnp.int32)
    second_idx = (first_idx + offset) % F1
    operator_id = jax.random.randint(keys[2], (P_SIZE,), 0, 4, jnp.int32)
    return jnp.stack([first_idx, second_idx, operator_id], axis=0).astype(jnp.int32)


def block_levels(rng, dims, pieces, smallest, top_value):
    factor_of = 1.0
    for position, blocks in pieces:
        heights = jax.random.uniform(jax.random.fold_in(jax.random.fold_in(rng, 6), position), (blocks,), jnp.float32, smallest / len(pieces), top_value / len(pieces))
        factor_of = factor_of * jnp.repeat(jnp.exp(heights), dims[position] // blocks).reshape((-1,) + (1,) * (len(dims) - 1 - position))
    return factor_of


def bell_draw(own_key, dims, width, reach, cuts=(), held_as=jnp.bfloat16):
    entries = jax.random.normal(own_key, dims, jnp.float32) * width
    if len(cuts) > 0:
        entries = block_levels(own_key, dims, cuts, -0.22, 0.18) * entries
    return jnp.clip(entries, min=-reach, max=reach).astype(held_as)


def setup_inputs(seed: int = 0) -> dict:
    seeds = jax.random.split(jax.random.key(seed), 4)
    tier_one = draw_tier_one(jax.random.fold_in(seeds[3], 71), 0)
    residuals = bell_draw(seeds[1], (SAMPLES, K), 1.0, 6.0, ((0, 8),))
    pair_list = draw_pair_list(jax.random.fold_in(seeds[3], 71), 0)
    return dict(tier_one=tier_one, residuals=residuals, pair_list=pair_list)


epsilon = 1e-05

def descriptors(tier_one, pair_cols):
    first_rows = jnp.take(tier_one, pair_cols[0], axis=0).astype(jnp.float32)
    second_rows = jnp.take(tier_one, pair_cols[1], axis=0).astype(jnp.float32)
    operator_id = pair_cols[2][:, None]
    quotient = first_rows / (1.0 + jnp.abs(second_rows))
    built = jnp.where(operator_id == 0, first_rows + second_rows, jnp.where(operator_id == 1, first_rows - second_rows, jnp.where(operator_id == 2, first_rows * second_rows, quotient)))
    return built.astype(jnp.bfloat16)

def block_terms(tier_one, residuals, pair_cols):
    built = descriptors(tier_one, pair_cols)
    product = jnp.dot(built, residuals, preferred_element_type=jnp.float32)
    widened = built.astype(jnp.float32)
    return (product, lax.optimization_barrier(jnp.sum(widened, axis=1)), lax.optimization_barrier(jnp.sum(widened * widened, axis=1)))

def finish(product, first_sums, square_sums, col_totals, sample_count):
    means = first_sums / sample_count
    variance = square_sums / sample_count - means * means
    centred = product - means[:, None] * col_totals[None, :]
    return centred * lax.rsqrt(variance + epsilon)[:, None] / math.sqrt(sample_count)

def reference(tier_one, residuals, pair_list):
    block_size = math.gcd(P_SIZE, 1024)
    block_count = P_SIZE // block_size
    grouped = pair_list.reshape(3, block_count, block_size).transpose(1, 0, 2)
    product, first_sums, square_sums = lax.map(lambda pair_cols: block_terms(tier_one, residuals, pair_cols), grouped)
    product = product.reshape(P_SIZE, K)
    first_sums = first_sums.reshape(P_SIZE)
    square_sums = square_sums.reshape(P_SIZE)
    col_totals = lax.optimization_barrier(jnp.sum(residuals.astype(jnp.float32), axis=0))
    return finish(product, first_sums, square_sums, col_totals, SAMPLES)
```

```python
import functools
import math

import jax
import jax.numpy as jnp
from jax import lax
from jax.experimental import pallas as pl
from jax.experimental.pallas import tpu as pltpu
from jax.sharding import PartitionSpec as P

epsilon = 1e-05
MESH = pl.DeviceIdType.MESH
lanes = 128


def kernel(
    sizes, tier_ref, res_ref, pair_smem, pair_vmem, out_ref,
    slots, table, first_stage, second_stage, op_wide, weights, send_block, recv_block,
    send_stats, recv_stats, turned,
    own_sem, cross_send, cross_recv, sib_send, sib_recv, relay_send, relay_recv,
    block_send, block_recv, stats_send, stats_recv,
):
    n_feat, n_samp, rows, samples, pairs, chunks = sizes
    chips = n_feat // 2
    pieces = samples // lanes
    owned = pairs // n_samp
    sub = min(owned, 256)
    step = rows // chunks
    total_samples = samples * n_samp
    feat = lax.axis_index("feat")
    samp = lax.axis_index("samp")
    chip = feat // 2
    core = lax.rem(feat, 2)
    sibling = chip * 2 + 1 - core

    def far(offset):
        return lax.rem(chip + offset, chips) * 2 + core

    barrier = pltpu.get_barrier_semaphore()
    pl.semaphore_signal(barrier, inc=1, device_id=(sibling, samp), device_id_type=MESH)
    for offset in range(1, chips):
        pl.semaphore_signal(barrier, inc=1, device_id=(far(offset), samp), device_id_type=MESH)
    for offset in range(1, n_samp):
        pl.semaphore_signal(
            barrier, inc=1, device_id=(feat, lax.rem(samp + offset, n_samp)), device_id_type=MESH
        )
    own_copy = pltpu.make_async_copy(tier_ref, slots.at[feat], own_sem)
    own_copy.start()
    pl.semaphore_wait(barrier, 1 + (chips - 1) + (n_samp - 1))

    def part(index):
        return pl.ds(pl.multiple_of(index * step, step), step)

    def cross(offset, k, holder, target):
        return pltpu.make_async_remote_copy(
            src_ref=tier_ref.at[part(k)],
            dst_ref=slots.at[holder, part(k)],
            send_sem=cross_send.at[offset - 1, k],
            recv_sem=cross_recv.at[offset - 1, k],
            device_id=(target, samp),
            device_id_type=MESH,
        )

    def relay(offset, k, holder):
        return pltpu.make_async_remote_copy(
            src_ref=slots.at[holder, part(k)],
            dst_ref=slots.at[holder, part(k)],
            send_sem=relay_send.at[offset - 1, k],
            recv_sem=relay_recv.at[offset - 1, k],
            device_id=(sibling, samp),
            device_id_type=MESH,
        )

    def to_sibling(holder):
        return pltpu.make_async_remote_copy(
            src_ref=tier_ref,
            dst_ref=slots.at[holder],
            send_sem=sib_send,
            recv_sem=sib_recv,
            device_id=(sibling, samp),
            device_id_type=MESH,
        )

    for offset in range(1, chips):
        @pl.loop(0, chunks)
        def _(k):
            cross(offset, k, feat, far(offset)).start()
    to_sibling(feat).start()

    flat = table.reshape(n_feat * rows * 4, lanes)

    def widen(holder, k):
        @pl.loop(0, step // 64 if step % 64 == 0 else 1)
        def _(g):
            size = 64 if step % 64 == 0 else step
            start = pl.multiple_of(k * step + g * size, size)
            for j in range(pieces):
                values = slots[holder, pl.ds(start, size), j * lanes:(j + 1) * lanes]
                flat[pl.ds(4 * (holder * rows + start) + j, size, stride=4), :] = values.astype(jnp.float32)

    weights[:, :lanes] = res_ref[...]
    weights[:, lanes:] = jnp.ones((samples, lanes), jnp.bfloat16)
    col_local = jnp.sum(res_ref[...].astype(jnp.float32), axis=0, keepdims=True)

    @pl.loop(0, pairs // lanes)
    def _(g):
        span = pl.ds(pl.multiple_of(g * lanes, lanes), lanes)
        op_wide[span, :] = jnp.broadcast_to(pair_vmem[2:3, span], (lanes, lanes)).T

    own_copy.wait()

    @pl.loop(0, chunks)
    def _(k):
        widen(feat, k)

    to_sibling(sibling).wait_recv()

    @pl.loop(0, chunks)
    def _(k):
        widen(sibling, k)

    for offset in range(1, chips):
        mine = far(chips - offset)
        theirs = mine + 1 - 2 * core

        @pl.loop(0, chunks)
        def _(k):
            cross(offset, k, mine, feat).wait_recv()
            relay(offset, k, mine).start()
            widen(mine, k)

            @pl.when(k > 0)
            def _():
                relay(offset, k - 1, theirs).wait_recv()
                widen(theirs, k - 1)

        relay(offset, chunks - 1, theirs).wait_recv()
        widen(theirs, chunks - 1)

    lane_id = lax.broadcasted_iota(jnp.int32, (sub, lanes), 1)

    def make_block(slot, owner):
        @pl.loop(0, owned // sub)
        def _(h):
            base = owner * owned + h * sub

            @pl.loop(0, sub // 16)
            def _(g):
                for u in range(16):
                    p = g * 16 + u
                    first = pair_smem[0, base + p]
                    second = pair_smem[1, base + p]
                    spot = pl.ds(pl.multiple_of(p * 4, 4), 4)
                    first_stage[spot, :] = table[first]
                    second_stage[spot, :] = table[second]

            op = op_wide[pl.ds(pl.multiple_of(base, sub), sub), :]
            parts = []
            square = jnp.zeros((sub, lanes), jnp.float32)
            for j in range(pieces):
                a = first_stage[pl.ds(j, sub, stride=4), :]
                b = second_stage[pl.ds(j, sub, stride=4), :]
                plain = a + jnp.where(op == 1, -b, b)
                other = jnp.where(op == 2, a * b, a / (1.0 + jnp.abs(b)))
                built = jnp.where(op < 2, plain, other).astype(jnp.bfloat16)
                parts.append(built)
                wide = built.astype(jnp.float32)
                square += wide * wide
            both = jnp.dot(
                jnp.concatenate(parts, axis=1), weights[...], preferred_element_type=jnp.float32
            )
            sums = both[:, lanes:]
            centred = both[:, :lanes] - sums * (col_local / samples)
            here = pl.ds(pl.multiple_of(h * sub, sub), sub)
            send_block[slot, here, :] = centred.astype(jnp.bfloat16)
            stats = jnp.where(lane_id == 0, sums, jnp.sum(square, axis=1, keepdims=True))
            for q in range(sub // lanes):
                flipped = stats[q * lanes:(q + 1) * lanes, :].T
                send_stats[slot, 0:2, pl.ds(pl.multiple_of(h * sub + q * lanes, lanes), lanes)] = flipped[0:2, :]
        send_stats[slot, 2:3, 0:lanes] = col_local

    def send_block_to(slot, source, target):
        return pltpu.make_async_remote_copy(
            src_ref=send_block.at[slot],
            dst_ref=recv_block.at[source],
            send_sem=block_send.at[slot],
            recv_sem=block_recv.at[source],
            device_id=(feat, target),
            device_id_type=MESH,
        )

    def send_stats_to(slot, source, target):
        return pltpu.make_async_remote_copy(
            src_ref=send_stats.at[slot],
            dst_ref=recv_stats.at[source],
            send_sem=stats_send.at[slot],
            recv_sem=stats_recv.at[source],
            device_id=(feat, target),
            device_id_type=MESH,
        )

    @pl.loop(0, n_samp)
    def _(t):
        owner = lax.rem(samp + 1 + t, n_samp)
        make_block(t, owner)

        @pl.when(t < n_samp - 1)
        def _():
            send_block_to(t, samp, owner).start()
            send_stats_to(t, samp, owner).start()

    recv_stats[samp] = send_stats[n_samp - 1]
    out_ref[...] = send_block[n_samp - 1].astype(jnp.float32)

    @pl.loop(0, n_samp - 1)
    def _(t):
        source = lax.rem(samp + n_samp - 1 - t, n_samp)
        send_block_to(t, source, samp).wait_recv()
        send_stats_to(t, source, samp).wait_recv()
        out_ref[...] += recv_block[source].astype(jnp.float32)

    first_sums = jnp.zeros((1, owned), jnp.float32)
    square_sums = jnp.zeros((1, owned), jnp.float32)
    for d in range(n_samp):
        first_sums += recv_stats[d, 0:1, :]
        square_sums += recv_stats[d, 1:2, :]
    means = first_sums / total_samples
    variance = square_sums / total_samples - means * means
    turned[n_samp:n_samp + 1, :] = lax.rsqrt(variance + epsilon) / math.sqrt(total_samples)
    for d in range(n_samp):
        turned[d:d + 1, :] = recv_stats[d, 0:1, :] / samples - means

    @pl.loop(0, owned // lanes)
    def _(q):
        span = pl.ds(pl.multiple_of(q * lanes, lanes), lanes)
        columns = turned[:, span].T
        total = out_ref[span, :]
        for d in range(n_samp):
            total += columns[:, d:d + 1] * recv_stats[d, 2:3, 0:lanes]
        out_ref[span, :] = total * columns[:, n_samp:n_samp + 1]

    to_sibling(feat).wait_send()
    for offset in range(1, chips):
        @pl.loop(0, chunks)
        def _(k):
            cross(offset, k, feat, far(offset)).wait_send()
            relay(offset, k, far(chips - offset)).wait_send()

    @pl.loop(0, n_samp - 1)
    def _(t):
        owner = lax.rem(samp + 1 + t, n_samp)
        send_block_to(t, samp, owner).wait_send()
        send_stats_to(t, samp, owner).wait_send()


def per_device(n_feat, n_samp, tier_one, residuals, pair_list):
    rows, samples = tier_one.shape
    pairs = pair_list.shape[1]
    chips = n_feat // 2
    owned = pairs // n_samp
    sub = min(owned, 256)
    chunks = 8
    sizes = (n_feat, n_samp, rows, samples, pairs, chunks)
    dma = pltpu.SemaphoreType.DMA
    return pl.pallas_call(
        functools.partial(kernel, sizes),
        out_shape=jax.ShapeDtypeStruct((owned, lanes), jnp.float32),
        in_specs=[
            pl.BlockSpec(memory_space=pl.ANY),
            pl.BlockSpec(memory_space=pltpu.VMEM),
            pl.BlockSpec(memory_space=pltpu.SMEM),
            pl.BlockSpec(memory_space=pltpu.VMEM),
        ],
        out_specs=pl.BlockSpec(memory_space=pltpu.VMEM),
        scratch_shapes=[
            pltpu.VMEM((n_feat, rows, samples), jnp.bfloat16),
            pltpu.VMEM((n_feat * rows, 4, lanes), jnp.float32),
            pltpu.VMEM((sub * 4, lanes), jnp.float32),
            pltpu.VMEM((sub * 4, lanes), jnp.float32),
            pltpu.VMEM((pairs, lanes), jnp.int32),
            pltpu.VMEM((samples, 2 * lanes), jnp.bfloat16),
            pltpu.VMEM((n_samp, owned, lanes), jnp.bfloat16),
            pltpu.VMEM((n_samp, owned, lanes), jnp.bfloat16),
            pltpu.VMEM((n_samp, 8, owned), jnp.float32),
            pltpu.VMEM((n_samp, 8, owned), jnp.float32),
            pltpu.VMEM((lanes, owned), jnp.float32),
            dma,
            dma((max(chips - 1, 1), chunks)),
            dma((max(chips - 1, 1), chunks)),
            dma,
            dma,
            dma((max(chips - 1, 1), chunks)),
            dma((max(chips - 1, 1), chunks)),
            dma((n_samp,)),
            dma((n_samp,)),
            dma((n_samp,)),
            dma((n_samp,)),
        ],
        compiler_params=pltpu.CompilerParams(
            collective_id=0, has_side_effects=True, vmem_limit_bytes=56 * 2**20
        ),
    )(tier_one, residuals, pair_list, pair_list)


def solution(mesh):
    in_specs = (P("feat", "samp"), P("samp", None), P(None, "feat"))
    out_specs = P(("feat", "samp"), None)
    return jax.shard_map(
        functools.partial(per_device, mesh.shape["feat"], mesh.shape["samp"]),
        mesh=mesh, in_specs=in_specs, out_specs=out_specs, check_vma=False,
    )
```

```python
import functools
import math

import jax
import jax.numpy as jnp
from jax import lax
from jax.experimental import pallas as pl
from jax.experimental.pallas import tpu as pltpu
from jax.sharding import PartitionSpec as P

epsilon = 1e-05
MESH = pl.DeviceIdType.MESH
lanes = 128


def kernel(
    sizes, tier_ref, res_ref, pair_smem, pair_vmem, out_ref,
    slots, table, first_stage, second_stage, op_wide, weights,
    near_out, near_in, line_out, line_in, send_stats, recv_stats, turned, scale,
    own_sem, cross_send, cross_recv, sib_send, sib_recv, relay_send, relay_recv,
    near_send, near_recv, line_send, line_recv, stats_send, stats_recv,
):
    n_feat, n_samp, rows, samples, pairs, chunks = sizes
    chips = n_feat // 2
    pieces = samples // lanes
    owned = pairs // n_samp
    sub = min(owned, 256)
    step = rows // chunks
    total_samples = samples * n_samp
    feat = lax.axis_index("feat")
    samp = lax.axis_index("samp")
    chip = feat // 2
    core = lax.rem(feat, 2)
    sibling = chip * 2 + 1 - core
    half = n_samp // 2
    high = samp // 2
    low = lax.rem(samp, 2)
    partner = high * 2 + 1 - low

    def far(offset):
        return lax.rem(chip + offset, chips) * 2 + core

    barrier = pltpu.get_barrier_semaphore()
    pl.semaphore_signal(barrier, inc=1, device_id=(sibling, samp), device_id_type=MESH)
    for offset in range(1, chips):
        pl.semaphore_signal(barrier, inc=1, device_id=(far(offset), samp), device_id_type=MESH)
    for offset in range(1, n_samp):
        pl.semaphore_signal(
            barrier, inc=1, device_id=(feat, lax.rem(samp + offset, n_samp)), device_id_type=MESH
        )
    own_copy = pltpu.make_async_copy(tier_ref, slots.at[feat], own_sem)
    own_copy.start()
    pl.semaphore_wait(barrier, 1 + (chips - 1) + (n_samp - 1))

    def part(index):
        return pl.ds(pl.multiple_of(index * step, step), step)

    def cross(offset, k, holder, target):
        return pltpu.make_async_remote_copy(
            src_ref=tier_ref.at[part(k)],
            dst_ref=slots.at[holder, part(k)],
            send_sem=cross_send.at[offset - 1, k],
            recv_sem=cross_recv.at[offset - 1, k],
            device_id=(target, samp),
            device_id_type=MESH,
        )

    def relay(offset, k, holder):
        return pltpu.make_async_remote_copy(
            src_ref=slots.at[holder, part(k)],
            dst_ref=slots.at[holder, part(k)],
            send_sem=relay_send.at[offset - 1, k],
            recv_sem=relay_recv.at[offset - 1, k],
            device_id=(sibling, samp),
            device_id_type=MESH,
        )

    def to_sibling(holder):
        return pltpu.make_async_remote_copy(
            src_ref=tier_ref,
            dst_ref=slots.at[holder],
            send_sem=sib_send,
            recv_sem=sib_recv,
            device_id=(sibling, samp),
            device_id_type=MESH,
        )

    for offset in range(1, chips):
        @pl.loop(0, chunks)
        def _(k):
            cross(offset, k, feat, far(offset)).start()
    to_sibling(feat).start()

    flat = table.reshape(n_feat * rows * 4, lanes)

    def widen(holder, k):
        @pl.loop(0, step // 64 if step % 64 == 0 else 1)
        def _(g):
            size = 64 if step % 64 == 0 else step
            start = pl.multiple_of(k * step + g * size, size)
            for j in range(pieces):
                values = slots[holder, pl.ds(start, size), j * lanes:(j + 1) * lanes]
                flat[pl.ds(4 * (holder * rows + start) + j, size, stride=4), :] = values.astype(jnp.float32)

    weights[:, :lanes] = res_ref[...]
    weights[:, lanes:] = jnp.ones((samples, lanes), jnp.bfloat16)
    col_local = jnp.sum(res_ref[...].astype(jnp.float32), axis=0, keepdims=True)

    @pl.loop(0, pairs // lanes)
    def _(g):
        span = pl.ds(pl.multiple_of(g * lanes, lanes), lanes)
        op_wide[span, :] = jnp.broadcast_to(pair_vmem[2:3, span], (lanes, lanes)).T

    own_copy.wait()

    @pl.loop(0, chunks)
    def _(k):
        widen(feat, k)

    to_sibling(sibling).wait_recv()

    @pl.loop(0, chunks)
    def _(k):
        widen(sibling, k)

    for offset in range(1, chips):
        mine = far(chips - offset)
        theirs = mine + 1 - 2 * core

        @pl.loop(0, chunks)
        def _(k):
            cross(offset, k, mine, feat).wait_recv()
            relay(offset, k, mine).start()
            widen(mine, k)

            @pl.when(k > 0)
            def _():
                relay(offset, k - 1, theirs).wait_recv()
                widen(theirs, k - 1)

        relay(offset, chunks - 1, theirs).wait_recv()
        widen(theirs, chunks - 1)

    lane_id = lax.broadcasted_iota(jnp.int32, (sub, lanes), 1)

    def make_block(owner, keep):
        @pl.loop(0, owned // sub)
        def _(h):
            base = owner * owned + h * sub

            @pl.loop(0, sub // 16)
            def _(g):
                firsts = [table[pair_smem[0, base + g * 16 + u]] for u in range(16)]
                seconds = [table[pair_smem[1, base + g * 16 + u]] for u in range(16)]
                for u in range(16):
                    spot = pl.ds(pl.multiple_of((g * 16 + u) * 4, 4), 4)
                    first_stage[spot, :] = firsts[u]
                    second_stage[spot, :] = seconds[u]

            op = op_wide[pl.ds(pl.multiple_of(base, sub), sub), :]
            parts = []
            square = jnp.zeros((sub, lanes), jnp.float32)
            for j in range(pieces):
                a = first_stage[pl.ds(j, sub, stride=4), :]
                b = second_stage[pl.ds(j, sub, stride=4), :]
                plain = a + jnp.where(op == 1, -b, b)
                other = jnp.where(op == 2, a * b, a / (1.0 + jnp.abs(b)))
                built = jnp.where(op < 2, plain, other).astype(jnp.bfloat16)
                parts.append(built)
                wide = built.astype(jnp.float32)
                square += wide * wide
            both = jnp.dot(
                jnp.concatenate(parts, axis=1), weights[...], preferred_element_type=jnp.float32
            )
            sums = both[:, lanes:]
            centred = both[:, :lanes] - sums * (col_local / samples)
            keep(pl.ds(pl.multiple_of(h * sub, sub), sub), centred)
            stats = jnp.where(lane_id == 0, sums, jnp.sum(square, axis=1, keepdims=True))
            for q in range(sub // lanes):
                flipped = stats[q * lanes:(q + 1) * lanes, :].T
                send_stats[owner, 0:2, pl.ds(pl.multiple_of(h * sub + q * lanes, lanes), lanes)] = flipped[0:2, :]
        send_stats[owner, 2:3, 0:lanes] = col_local

    def near_copy(t):
        return pltpu.make_async_remote_copy(
            src_ref=near_out.at[t],
            dst_ref=near_in.at[t],
            send_sem=near_send.at[t],
            recv_sem=near_recv.at[t],
            device_id=(feat, partner),
            device_id_type=MESH,
        )

    def line_copy(t, source, target):
        return pltpu.make_async_remote_copy(
            src_ref=line_out.at[t],
            dst_ref=line_in.at[source],
            send_sem=line_send.at[t],
            recv_sem=line_recv.at[source],
            device_id=(feat, target * 2 + low),
            device_id_type=MESH,
        )

    def stats_copy(owner, source):
        return pltpu.make_async_remote_copy(
            src_ref=send_stats.at[owner],
            dst_ref=recv_stats.at[source],
            send_sem=stats_send.at[owner],
            recv_sem=stats_recv.at[source],
            device_id=(feat, owner),
            device_id_type=MESH,
        )

    @pl.loop(0, half + 1)
    def _(t):
        @pl.when(t < half)
        def _():
            owner = lax.rem(high + 1 + t, half) * 2 + 1 - low

            def keep(here, centred):
                near_out[t, here, :] = centred.astype(jnp.bfloat16)

            make_block(owner, keep)
            near_copy(t).start()
            stats_copy(owner, samp).start()

        @pl.when(t > 0)
        def _():
            target = lax.rem(high + t, half)
            owner = target * 2 + low
            near_copy(t - 1).wait_recv()

            def keep(here, centred):
                total = centred + near_in[t - 1, here, :].astype(jnp.float32)
                line_out[t - 1, here, :] = total.astype(jnp.bfloat16)
                out_ref[here, :] = total

            make_block(owner, keep)

            @pl.when(t < half)
            def _():
                line_copy(t - 1, high, target).start()
                stats_copy(owner, samp).start()

    recv_stats[samp] = send_stats[samp]

    @pl.loop(1, n_samp)
    def _(t):
        stats_copy(samp, lax.rem(samp + n_samp - t, n_samp)).wait_recv()

    first_sums = jnp.zeros((1, owned), jnp.float32)
    square_sums = jnp.zeros((1, owned), jnp.float32)
    for d in range(n_samp):
        first_sums += recv_stats[d, 0:1, :]
        square_sums += recv_stats[d, 1:2, :]
    means = first_sums / total_samples
    variance = square_sums / total_samples - means * means
    turned[n_samp:n_samp + 1, :] = lax.rsqrt(variance + epsilon) / math.sqrt(total_samples)
    for d in range(n_samp):
        turned[d:d + 1, :] = recv_stats[d, 0:1, :] / samples - means

    @pl.loop(0, owned // lanes)
    def _(q):
        span = pl.ds(pl.multiple_of(q * lanes, lanes), lanes)
        columns = turned[:, span].T
        total = out_ref[span, :]
        for d in range(n_samp):
            total += columns[:, d:d + 1] * recv_stats[d, 2:3, 0:lanes]
        out_ref[span, :] = total
        scale[span, :] = jnp.broadcast_to(columns[:, n_samp:n_samp + 1], (lanes, lanes))

    @pl.loop(0, half - 1)
    def _(t):
        source = lax.rem(high + half - 1 - t, half)
        line_copy(t, source, high).wait_recv()
        out_ref[...] += line_in[source].astype(jnp.float32)

    out_ref[...] *= scale[...]

    to_sibling(feat).wait_send()
    for offset in range(1, chips):
        @pl.loop(0, chunks)
        def _(k):
            cross(offset, k, feat, far(offset)).wait_send()
            relay(offset, k, far(chips - offset)).wait_send()

    @pl.loop(0, half)
    def _(t):
        near_copy(t).wait_send()

        @pl.when(t < half - 1)
        def _():
            line_copy(t, high, lax.rem(high + 1 + t, half)).wait_send()

    @pl.loop(1, n_samp)
    def _(t):
        stats_copy(lax.rem(samp + t, n_samp), samp).wait_send()


def per_device(n_feat, n_samp, tier_one, residuals, pair_list):
    rows, samples = tier_one.shape
    pairs = pair_list.shape[1]
    chips = n_feat // 2
    owned = pairs // n_samp
    sub = min(owned, 256)
    chunks = 8
    sizes = (n_feat, n_samp, rows, samples, pairs, chunks)
    dma = pltpu.SemaphoreType.DMA
    return pl.pallas_call(
        functools.partial(kernel, sizes),
        out_shape=jax.ShapeDtypeStruct((owned, lanes), jnp.float32),
        in_specs=[
            pl.BlockSpec(memory_space=pl.ANY),
            pl.BlockSpec(memory_space=pltpu.VMEM),
            pl.BlockSpec(memory_space=pltpu.SMEM),
            pl.BlockSpec(memory_space=pltpu.VMEM),
        ],
        out_specs=pl.BlockSpec(memory_space=pltpu.VMEM),
        scratch_shapes=[
            pltpu.VMEM((n_feat, rows, samples), jnp.bfloat16),
            pltpu.VMEM((n_feat * rows, 4, lanes), jnp.float32),
            pltpu.VMEM((sub * 4, lanes), jnp.float32),
            pltpu.VMEM((sub * 4, lanes), jnp.float32),
            pltpu.VMEM((pairs, lanes), jnp.int32),
            pltpu.VMEM((samples, 2 * lanes), jnp.bfloat16),
            pltpu.VMEM((n_samp // 2, owned, lanes), jnp.bfloat16),
            pltpu.VMEM((n_samp // 2, owned, lanes), jnp.bfloat16),
            pltpu.VMEM((n_samp // 2, owned, lanes), jnp.bfloat16),
            pltpu.VMEM((n_samp // 2, owned, lanes), jnp.bfloat16),
            pltpu.VMEM((n_samp, 4, owned), jnp.float32),
            pltpu.VMEM((n_samp, 4, owned), jnp.float32),
            pltpu.VMEM((lanes, owned), jnp.float32),
            pltpu.VMEM((owned, lanes), jnp.float32),
            dma,
            dma((max(chips - 1, 1), chunks)),
            dma((max(chips - 1, 1), chunks)),
            dma,
            dma,
            dma((max(chips - 1, 1), chunks)),
            dma((max(chips - 1, 1), chunks)),
            dma((n_samp // 2,)),
            dma((n_samp // 2,)),
            dma((n_samp // 2,)),
            dma((n_samp // 2,)),
            dma((n_samp,)),
            dma((n_samp,)),
        ],
        compiler_params=pltpu.CompilerParams(
            collective_id=0, has_side_effects=True, vmem_limit_bytes=56 * 2**20
        ),
    )(tier_one, residuals, pair_list, pair_list)


def solution(mesh):
    in_specs = (P("feat", "samp"), P("samp", None), P(None, "feat"))
    out_specs = P(("feat", "samp"), None)
    return jax.shard_map(
        functools.partial(per_device, mesh.shape["feat"], mesh.shape["samp"]),
        mesh=mesh, in_specs=in_specs, out_specs=out_specs, check_vma=False,
    )
```

```python
import functools
import math

import jax
import jax.numpy as jnp
from jax import lax
from jax.experimental import pallas as pl
from jax.experimental.pallas import tpu as pltpu
from jax.sharding import PartitionSpec as P

epsilon = 1e-05
MESH = pl.DeviceIdType.MESH
lanes = 128


def kernel(
    sizes, tier_ref, res_ref, pair_smem, pair_vmem, out_ref,
    slots, table, first_even, second_even, first_odd, second_odd,
    op_wide, weights, share_block, stats_wide,
    near_out, near_in, line_out, line_in, send_stats, recv_stats, turned, scale,
    own_sem, cross_send, cross_recv, sib_send, sib_recv, relay_send, relay_recv,
    near_send, near_recv, line_send, line_recv, stats_send, stats_recv,
):
    n_feat, n_samp, rows, samples, pairs, chunks = sizes
    chips = n_feat // 2
    pieces = samples // lanes
    owned = pairs // n_samp
    sub = min(owned // 2, 128)
    group, tall = 8, 16
    step = rows // chunks
    total_samples = samples * n_samp
    feat = lax.axis_index("feat")
    samp = lax.axis_index("samp")
    chip = feat // 2
    core = lax.rem(feat, 2)
    sibling = chip * 2 + 1 - core
    half = n_samp // 2
    high = samp // 2
    low = lax.rem(samp, 2)
    partner = high * 2 + 1 - low

    def far(offset):
        return lax.rem(chip + offset, chips) * 2 + core

    barrier = pltpu.get_barrier_semaphore()
    pl.semaphore_signal(barrier, inc=1, device_id=(sibling, samp), device_id_type=MESH)
    for offset in range(1, chips):
        pl.semaphore_signal(barrier, inc=1, device_id=(far(offset), samp), device_id_type=MESH)
    for offset in range(1, n_samp):
        pl.semaphore_signal(
            barrier, inc=1, device_id=(feat, lax.rem(samp + offset, n_samp)), device_id_type=MESH
        )
    own_copy = pltpu.make_async_copy(tier_ref, slots.at[feat], own_sem)
    own_copy.start()
    pl.semaphore_wait(barrier, 1 + (chips - 1) + (n_samp - 1))

    def part(index):
        return pl.ds(pl.multiple_of(index * step, step), step)

    def cross(offset, k, holder, target):
        return pltpu.make_async_remote_copy(
            src_ref=tier_ref.at[part(k)],
            dst_ref=slots.at[holder, part(k)],
            send_sem=cross_send.at[offset - 1, k],
            recv_sem=cross_recv.at[offset - 1, k],
            device_id=(target, samp),
            device_id_type=MESH,
        )

    def relay(offset, k, holder):
        return pltpu.make_async_remote_copy(
            src_ref=slots.at[holder, part(k)],
            dst_ref=slots.at[holder, part(k)],
            send_sem=relay_send.at[offset - 1, k],
            recv_sem=relay_recv.at[offset - 1, k],
            device_id=(sibling, samp),
            device_id_type=MESH,
        )

    def to_sibling(holder):
        return pltpu.make_async_remote_copy(
            src_ref=tier_ref,
            dst_ref=slots.at[holder],
            send_sem=sib_send,
            recv_sem=sib_recv,
            device_id=(sibling, samp),
            device_id_type=MESH,
        )

    for offset in range(1, chips):
        @pl.loop(0, chunks)
        def _(k):
            cross(offset, k, feat, far(offset)).start()
    to_sibling(feat).start()

    flat = table.reshape(n_feat * rows * 4, lanes)

    def widen(holder, k):
        @pl.loop(0, step // 64 if step % 64 == 0 else 1)
        def _(g):
            size = 64 if step % 64 == 0 else step
            start = pl.multiple_of(k * step + g * size, size)
            for j in range(pieces):
                values = slots[holder, pl.ds(start, size), j * lanes:(j + 1) * lanes]
                flat[pl.ds(4 * (holder * rows + start) + j, size, stride=4), :] = values.astype(jnp.float32)

    weights[:, :lanes] = res_ref[...]
    weights[:, lanes:] = jnp.ones((samples, lanes), jnp.bfloat16)
    col_local = jnp.sum(res_ref[...].astype(jnp.float32), axis=0, keepdims=True)

    @pl.loop(0, pairs // lanes)
    def _(g):
        span = pl.ds(pl.multiple_of(g * lanes, lanes), lanes)
        op_wide[span, :] = jnp.broadcast_to(pair_vmem[2:3, span], (lanes, lanes)).T

    own_copy.wait()

    @pl.loop(0, chunks)
    def _(k):
        widen(feat, k)

    to_sibling(sibling).wait_recv()

    @pl.loop(0, chunks)
    def _(k):
        widen(sibling, k)

    for offset in range(1, chips):
        mine = far(chips - offset)
        theirs = mine + 1 - 2 * core

        @pl.loop(0, chunks)
        def _(k):
            cross(offset, k, mine, feat).wait_recv()
            relay(offset, k, mine).start()
            widen(mine, k)

            @pl.when(k > 0)
            def _():
                relay(offset, k - 1, theirs).wait_recv()
                widen(theirs, k - 1)

        relay(offset, chunks - 1, theirs).wait_recv()
        widen(theirs, chunks - 1)

    lane_id = lax.broadcasted_iota(jnp.int32, (sub, lanes), 1)

    def owner_of(b):
        return lax.rem(high + 1 + b, half) * 2 + lax.rem(low + 1 + b // half, 2)

    def gather(stages, base, p):
        firsts = [table[pair_smem[0, base + p + u]] for u in range(group)]
        seconds = [table[pair_smem[1, base + p + u]] for u in range(group)]
        for u in range(group):
            stages[0][4 * (p + u):4 * (p + u) + 4, :] = firsts[u]
            stages[1][4 * (p + u):4 * (p + u) + 4, :] = seconds[u]

    def build(stages, base, p):
        op = op_wide[pl.ds(pl.multiple_of(base + p, tall), tall), :]
        parts = []
        square = jnp.zeros((tall, lanes), jnp.float32)
        for j in range(pieces):
            a = stages[0][pl.ds(4 * p + j, tall, stride=4), :]
            b = stages[1][pl.ds(4 * p + j, tall, stride=4), :]
            plain = a + jnp.where(op == 1, -b, b)
            other = jnp.where(op == 2, a * b, a / (1.0 + jnp.abs(b)))
            built = jnp.where(op < 2, plain, other).astype(jnp.bfloat16)
            parts.append(built)
            wide = built.astype(jnp.float32)
            square += wide * wide
        return jnp.concatenate(parts, axis=1), jnp.sum(square, axis=1, keepdims=True)

    def advance(now, base, later, next_base, here):
        built, squares = [], []
        steps = sub // tall
        share = sub // 2 // steps
        for i in range(steps):
            one, square = build(now, base, i * tall)
            built.append(one)
            squares.append(square)
            for p in range(i * share, (i + 1) * share, group):
                gather(later, next_base, p)
        both = jnp.dot(
            jnp.concatenate(built, axis=0), weights[...], preferred_element_type=jnp.float32
        )
        for p in range(sub // 2, sub, group):
            gather(later, next_base, p)
        sums = both[:, lanes:]
        share_block[here, :] = both[:, :lanes] - sums * (col_local / samples)
        stats_wide[here, :] = jnp.where(lane_id == 0, sums, jnp.concatenate(squares, axis=0))

    even = (first_even, second_even)
    odd = (first_odd, second_odd)

    @pl.loop(0, sub // group)
    def _(g):
        base = owner_of(0) * owned
        firsts = [table[pair_smem[0, base + g * group + u]] for u in range(group)]
        seconds = [table[pair_smem[1, base + g * group + u]] for u in range(group)]
        for u in range(group):
            spot = pl.ds(pl.multiple_of((g * group + u) * 4, 4), 4)
            first_even[spot, :] = firsts[u]
            second_even[spot, :] = seconds[u]

    couples = owned // (2 * sub)

    def make_block(b, owner):
        @pl.loop(0, couples)
        def _(h):
            base = owner * owned + h * (2 * sub)
            after = b * couples + h + 1
            next_base = owner_of(after // couples) * owned + lax.rem(after, couples) * (2 * sub)
            first_half = pl.ds(pl.multiple_of(h * (2 * sub), sub), sub)
            second_half = pl.ds(pl.multiple_of(h * (2 * sub) + sub, sub), sub)
            advance(even, base, odd, base + sub, first_half)
            advance(odd, base + sub, even, next_base, second_half)

        for q in range(owned // lanes):
            flipped = stats_wide[q * lanes:(q + 1) * lanes, :].T
            send_stats[owner, 0:2, q * lanes:(q + 1) * lanes] = flipped[0:2, :]
        send_stats[owner, 2:3, 0:lanes] = col_local

    def near_copy(t):
        return pltpu.make_async_remote_copy(
            src_ref=near_out.at[t],
            dst_ref=near_in.at[t],
            send_sem=near_send.at[t],
            recv_sem=near_recv.at[t],
            device_id=(feat, partner),
            device_id_type=MESH,
        )

    def line_copy(t, source, target):
        return pltpu.make_async_remote_copy(
            src_ref=line_out.at[t],
            dst_ref=line_in.at[source],
            send_sem=line_send.at[t],
            recv_sem=line_recv.at[source],
            device_id=(feat, target * 2 + low),
            device_id_type=MESH,
        )

    def stats_copy(owner, source):
        return pltpu.make_async_remote_copy(
            src_ref=send_stats.at[owner],
            dst_ref=recv_stats.at[source],
            send_sem=stats_send.at[owner],
            recv_sem=stats_recv.at[source],
            device_id=(feat, owner),
            device_id_type=MESH,
        )

    @pl.loop(0, n_samp)
    def _(b):
        owner = owner_of(b)
        make_block(b, owner)

        @pl.when(b < half)
        def _():
            near_out[b] = share_block[...].astype(jnp.bfloat16)
            near_copy(b).start()
            stats_copy(owner, samp).start()

        @pl.when(b >= half)
        def _():
            t = b - half
            near_copy(t).wait_recv()
            total = share_block[...] + near_in[t].astype(jnp.float32)
            line_out[t] = total.astype(jnp.bfloat16)
            out_ref[...] = total

            @pl.when(t < half - 1)
            def _():
                line_copy(t, high, lax.rem(high + 1 + t, half)).start()
                stats_copy(owner, samp).start()

    recv_stats[samp] = send_stats[samp]

    @pl.loop(1, n_samp)
    def _(t):
        stats_copy(samp, lax.rem(samp + n_samp - t, n_samp)).wait_recv()

    first_sums = jnp.zeros((1, owned), jnp.float32)
    square_sums = jnp.zeros((1, owned), jnp.float32)
    for d in range(n_samp):
        first_sums += recv_stats[d, 0:1, :]
        square_sums += recv_stats[d, 1:2, :]
    means = first_sums / total_samples
    variance = square_sums / total_samples - means * means
    turned[n_samp:n_samp + 1, :] = lax.rsqrt(variance + epsilon) / math.sqrt(total_samples)
    for d in range(n_samp):
        turned[d:d + 1, :] = recv_stats[d, 0:1, :] / samples - means

    @pl.loop(0, owned // lanes)
    def _(q):
        span = pl.ds(pl.multiple_of(q * lanes, lanes), lanes)
        columns = turned[:, span].T
        total = out_ref[span, :]
        for d in range(n_samp):
            total += columns[:, d:d + 1] * recv_stats[d, 2:3, 0:lanes]
        out_ref[span, :] = total
        scale[span, :] = jnp.broadcast_to(columns[:, n_samp:n_samp + 1], (lanes, lanes))

    @pl.loop(0, half - 1)
    def _(t):
        source = lax.rem(high + half - 1 - t, half)
        line_copy(t, source, high).wait_recv()
        out_ref[...] += line_in[source].astype(jnp.float32)

    out_ref[...] *= scale[...]

    to_sibling(feat).wait_send()
    for offset in range(1, chips):
        @pl.loop(0, chunks)
        def _(k):
            cross(offset, k, feat, far(offset)).wait_send()
            relay(offset, k, far(chips - offset)).wait_send()

    @pl.loop(0, half)
    def _(t):
        near_copy(t).wait_send()

        @pl.when(t < half - 1)
        def _():
            line_copy(t, high, lax.rem(high + 1 + t, half)).wait_send()

    @pl.loop(1, n_samp)
    def _(t):
        stats_copy(lax.rem(samp + t, n_samp), samp).wait_send()


def per_device(n_feat, n_samp, tier_one, residuals, pair_list):
    rows, samples = tier_one.shape
    pairs = pair_list.shape[1]
    chips = n_feat // 2
    owned = pairs // n_samp
    sub = min(owned // 2, 128)
    chunks = 8
    sizes = (n_feat, n_samp, rows, samples, pairs, chunks)
    dma = pltpu.SemaphoreType.DMA
    return pl.pallas_call(
        functools.partial(kernel, sizes),
        out_shape=jax.ShapeDtypeStruct((owned, lanes), jnp.float32),
        in_specs=[
            pl.BlockSpec(memory_space=pl.ANY),
            pl.BlockSpec(memory_space=pltpu.VMEM),
            pl.BlockSpec(memory_space=pltpu.SMEM),
            pl.BlockSpec(memory_space=pltpu.VMEM),
        ],
        out_specs=pl.BlockSpec(memory_space=pltpu.VMEM),
        scratch_shapes=[
            pltpu.VMEM((n_feat, rows, samples), jnp.bfloat16),
            pltpu.VMEM((n_feat * rows, 4, lanes), jnp.float32),
            pltpu.VMEM((sub * 4, lanes), jnp.float32),
            pltpu.VMEM((sub * 4, lanes), jnp.float32),
            pltpu.VMEM((sub * 4, lanes), jnp.float32),
            pltpu.VMEM((sub * 4, lanes), jnp.float32),
            pltpu.VMEM((pairs, lanes), jnp.int32),
            pltpu.VMEM((samples, 2 * lanes), jnp.bfloat16),
            pltpu.VMEM((owned, lanes), jnp.float32),
            pltpu.VMEM((owned, lanes), jnp.float32),
            pltpu.VMEM((n_samp // 2, owned, lanes), jnp.bfloat16),
            pltpu.VMEM((n_samp // 2, owned, lanes), jnp.bfloat16),
            pltpu.VMEM((n_samp // 2, owned, lanes), jnp.bfloat16),
            pltpu.VMEM((n_samp // 2, owned, lanes), jnp.bfloat16),
            pltpu.VMEM((n_samp, 4, owned), jnp.float32),
            pltpu.VMEM((n_samp, 4, owned), jnp.float32),
            pltpu.VMEM((lanes, owned), jnp.float32),
            pltpu.VMEM((owned, lanes), jnp.float32),
            dma,
            dma((max(chips - 1, 1), chunks)),
            dma((max(chips - 1, 1), chunks)),
            dma,
            dma,
            dma((max(chips - 1, 1), chunks)),
            dma((max(chips - 1, 1), chunks)),
            dma((n_samp // 2,)),
            dma((n_samp // 2,)),
            dma((n_samp // 2,)),
            dma((n_samp // 2,)),
            dma((n_samp,)),
            dma((n_samp,)),
        ],
        compiler_params=pltpu.CompilerParams(
            collective_id=0, has_side_effects=True, vmem_limit_bytes=56 * 2**20
        ),
    )(tier_one, residuals, pair_list, pair_list)


def solution(mesh):
    in_specs = (P("feat", "samp"), P("samp", None), P(None, "feat"))
    out_specs = P(("feat", "samp"), None)
    return jax.shard_map(
        functools.partial(per_device, mesh.shape["feat"], mesh.shape["samp"]),
        mesh=mesh, in_specs=in_specs, out_specs=out_specs, check_vma=False,
    )
```

```python
import functools
import math

import jax
import jax.numpy as jnp
from jax import lax
from jax.experimental import pallas as pl
from jax.experimental.pallas import tpu as pltpu
from jax.sharding import PartitionSpec as P

epsilon = 1e-05
MESH = pl.DeviceIdType.MESH
lanes = 128


def kernel(
    sizes, tier_ref, res_ref, pair_smem, pair_vmem, out_ref,
    slots, table, first_even, second_even, first_odd, second_odd,
    op_wide, weights, share_block, stats_wide,
    near_out, near_in, line_out, line_in, send_stats, recv_stats, turned, scale,
    own_sem, cross_send, cross_recv, sib_send, sib_recv, relay_send, relay_recv,
    near_send, near_recv, line_send, line_recv, stats_send, stats_recv,
):
    n_feat, n_samp, rows, samples, pairs, chunks = sizes
    chips = n_feat // 2
    pieces = samples // lanes
    owned = pairs // n_samp
    sub = min(owned // 2, 128)
    group, tall = 8, 16
    step = rows // chunks
    total_samples = samples * n_samp
    feat = lax.axis_index("feat")
    samp = lax.axis_index("samp")
    chip = feat // 2
    core = lax.rem(feat, 2)
    sibling = chip * 2 + 1 - core
    half = n_samp // 2
    high = samp // 2
    low = lax.rem(samp, 2)
    partner = high * 2 + 1 - low

    def far(offset):
        return lax.rem(chip + offset, chips) * 2 + core

    barrier = pltpu.get_barrier_semaphore()
    pl.semaphore_signal(barrier, inc=1, device_id=(sibling, samp), device_id_type=MESH)
    for offset in range(1, chips):
        pl.semaphore_signal(barrier, inc=1, device_id=(far(offset), samp), device_id_type=MESH)
    for offset in range(1, n_samp):
        pl.semaphore_signal(
            barrier, inc=1, device_id=(feat, lax.rem(samp + offset, n_samp)), device_id_type=MESH
        )
    own_copy = pltpu.make_async_copy(tier_ref, slots.at[feat], own_sem)
    own_copy.start()
    pl.semaphore_wait(barrier, 1 + (chips - 1) + (n_samp - 1))

    def part(index):
        return pl.ds(pl.multiple_of(index * step, step), step)

    def cross(offset, k, holder, target):
        return pltpu.make_async_remote_copy(
            src_ref=tier_ref.at[part(k)],
            dst_ref=slots.at[holder, part(k)],
            send_sem=cross_send.at[offset - 1, k],
            recv_sem=cross_recv.at[offset - 1, k],
            device_id=(target, samp),
            device_id_type=MESH,
        )

    def relay(offset, k, holder):
        return pltpu.make_async_remote_copy(
            src_ref=slots.at[holder, part(k)],
            dst_ref=slots.at[holder, part(k)],
            send_sem=relay_send.at[offset - 1, k],
            recv_sem=relay_recv.at[offset - 1, k],
            device_id=(sibling, samp),
            device_id_type=MESH,
        )

    def to_sibling(holder):
        return pltpu.make_async_remote_copy(
            src_ref=tier_ref,
            dst_ref=slots.at[holder],
            send_sem=sib_send,
            recv_sem=sib_recv,
            device_id=(sibling, samp),
            device_id_type=MESH,
        )

    for offset in range(1, chips):
        @pl.loop(0, chunks)
        def _(k):
            cross(offset, k, feat, far(offset)).start()
    to_sibling(feat).start()

    flat = table.reshape(n_feat * rows * 4, lanes)

    def widen(holder, k):
        @pl.loop(0, step // 64 if step % 64 == 0 else 1)
        def _(g):
            size = 64 if step % 64 == 0 else step
            start = pl.multiple_of(k * step + g * size, size)
            for j in range(pieces):
                values = slots[holder, pl.ds(start, size), j * lanes:(j + 1) * lanes]
                flat[pl.ds(4 * (holder * rows + start) + j, size, stride=4), :] = values.astype(jnp.float32)

    weights[:, :lanes] = res_ref[...]
    weights[:, lanes:] = jnp.ones((samples, lanes), jnp.bfloat16)
    col_local = jnp.sum(res_ref[...].astype(jnp.float32), axis=0, keepdims=True)

    @pl.loop(0, pairs // lanes)
    def _(g):
        span = pl.ds(pl.multiple_of(g * lanes, lanes), lanes)
        op_wide[span, :] = jnp.broadcast_to(pair_vmem[2:3, span], (lanes, lanes)).T

    own_copy.wait()

    @pl.loop(0, chunks)
    def _(k):
        widen(feat, k)

    to_sibling(sibling).wait_recv()

    @pl.loop(0, chunks)
    def _(k):
        widen(sibling, k)

    for offset in range(1, chips):
        mine = far(chips - offset)
        theirs = mine + 1 - 2 * core

        @pl.loop(0, chunks)
        def _(k):
            cross(offset, k, mine, feat).wait_recv()
            relay(offset, k, mine).start()
            widen(mine, k)

            @pl.when(k > 0)
            def _():
                relay(offset, k - 1, theirs).wait_recv()
                widen(theirs, k - 1)

        relay(offset, chunks - 1, theirs).wait_recv()
        widen(theirs, chunks - 1)

    lane_id = lax.broadcasted_iota(jnp.int32, (sub, lanes), 1)

    def owner_of(b):
        return lax.rem(high + 1 + b, half) * 2 + lax.rem(low + 1 + b // half, 2)

    def gather(stages, base, p):
        firsts = [table[pair_smem[base + (p + u)]] for u in range(group)]
        seconds = [table[pair_smem[base + (pairs + p + u)]] for u in range(group)]
        for u in range(group):
            stages[0][4 * (p + u):4 * (p + u) + 4, :] = firsts[u]
            stages[1][4 * (p + u):4 * (p + u) + 4, :] = seconds[u]

    def build(stages, base, p):
        op = op_wide[pl.ds(pl.multiple_of(base + p, tall), tall), :]
        parts = []
        square = jnp.zeros((tall, lanes), jnp.float32)
        for j in range(pieces):
            a = stages[0][pl.ds(4 * p + j, tall, stride=4), :]
            b = stages[1][pl.ds(4 * p + j, tall, stride=4), :]
            plain = a + jnp.where(op == 1, -b, b)
            other = jnp.where(op == 2, a * b, a / (1.0 + jnp.abs(b)))
            built = jnp.where(op < 2, plain, other).astype(jnp.bfloat16)
            parts.append(built)
            wide = built.astype(jnp.float32)
            square += wide * wide
        return jnp.concatenate(parts, axis=1), jnp.sum(square, axis=1, keepdims=True)

    def advance(now, base, later, next_base, here):
        built, squares = [], []
        steps = sub // tall
        share = sub // 2 // steps
        for i in range(steps):
            one, square = build(now, base, i * tall)
            built.append(one)
            squares.append(square)
            for p in range(i * share, (i + 1) * share, group):
                gather(later, next_base, p)
        both = jnp.dot(
            jnp.concatenate(built, axis=0), weights[...], preferred_element_type=jnp.float32
        )
        for p in range(sub // 2, sub, group):
            gather(later, next_base, p)
        sums = both[:, lanes:]
        share_block[here, :] = both[:, :lanes] - sums * (col_local / samples)
        stats_wide[here, :] = jnp.where(lane_id == 0, sums, jnp.concatenate(squares, axis=0))

    even = (first_even, second_even)
    odd = (first_odd, second_odd)

    @pl.loop(0, sub // group)
    def _(g):
        base = owner_of(0) * owned
        firsts = [table[pair_smem[base + g * group + u]] for u in range(group)]
        seconds = [table[pair_smem[base + g * group + (pairs + u)]] for u in range(group)]
        for u in range(group):
            spot = pl.ds(pl.multiple_of((g * group + u) * 4, 4), 4)
            first_even[spot, :] = firsts[u]
            second_even[spot, :] = seconds[u]

    couples = owned // (2 * sub)

    def make_block(b, owner):
        @pl.loop(0, couples)
        def _(h):
            base = owner * owned + h * (2 * sub)
            after = b * couples + h + 1
            next_base = owner_of(after // couples) * owned + lax.rem(after, couples) * (2 * sub)
            first_half = pl.ds(pl.multiple_of(h * (2 * sub), sub), sub)
            second_half = pl.ds(pl.multiple_of(h * (2 * sub) + sub, sub), sub)
            advance(even, base, odd, base + sub, first_half)
            advance(odd, base + sub, even, next_base, second_half)

        for q in range(owned // lanes):
            flipped = stats_wide[q * lanes:(q + 1) * lanes, :].T
            send_stats[owner, 0:2, q * lanes:(q + 1) * lanes] = flipped[0:2, :]
        send_stats[owner, 2:3, 0:lanes] = col_local

    def near_copy(t):
        return pltpu.make_async_remote_copy(
            src_ref=near_out.at[t],
            dst_ref=near_in.at[t],
            send_sem=near_send.at[t],
            recv_sem=near_recv.at[t],
            device_id=(feat, partner),
            device_id_type=MESH,
        )

    def line_copy(t, source, target):
        return pltpu.make_async_remote_copy(
            src_ref=line_out.at[t],
            dst_ref=line_in.at[source],
            send_sem=line_send.at[t],
            recv_sem=line_recv.at[source],
            device_id=(feat, target * 2 + low),
            device_id_type=MESH,
        )

    def stats_copy(owner, source):
        return pltpu.make_async_remote_copy(
            src_ref=send_stats.at[owner],
            dst_ref=recv_stats.at[source],
            send_sem=stats_send.at[owner],
            recv_sem=stats_recv.at[source],
            device_id=(feat, owner),
            device_id_type=MESH,
        )

    @pl.loop(0, n_samp)
    def _(b):
        owner = owner_of(b)
        make_block(b, owner)

        @pl.when(b < half)
        def _():
            near_out[b] = share_block[...].astype(jnp.bfloat16)
            near_copy(b).start()
            stats_copy(owner, samp).start()

        @pl.when(b >= half)
        def _():
            t = b - half
            near_copy(t).wait_recv()
            total = share_block[...] + near_in[t].astype(jnp.float32)
            line_out[t] = total.astype(jnp.bfloat16)
            out_ref[...] = total

            @pl.when(t < half - 1)
            def _():
                line_copy(t, high, lax.rem(high + 1 + t, half)).start()
                stats_copy(owner, samp).start()

    recv_stats[samp] = send_stats[samp]

    @pl.loop(1, n_samp)
    def _(t):
        stats_copy(samp, lax.rem(samp + n_samp - t, n_samp)).wait_recv()

    first_sums = jnp.zeros((1, owned), jnp.float32)
    square_sums = jnp.zeros((1, owned), jnp.float32)
    for d in range(n_samp):
        first_sums += recv_stats[d, 0:1, :]
        square_sums += recv_stats[d, 1:2, :]
    means = first_sums / total_samples
    variance = square_sums / total_samples - means * means
    turned[n_samp:n_samp + 1, :] = lax.rsqrt(variance + epsilon) / math.sqrt(total_samples)
    for d in range(n_samp):
        turned[d:d + 1, :] = recv_stats[d, 0:1, :] / samples - means

    @pl.loop(0, owned // lanes)
    def _(q):
        span = pl.ds(pl.multiple_of(q * lanes, lanes), lanes)
        columns = turned[:, span].T
        total = out_ref[span, :]
        for d in range(n_samp):
            total += columns[:, d:d + 1] * recv_stats[d, 2:3, 0:lanes]
        out_ref[span, :] = total
        scale[span, :] = jnp.broadcast_to(columns[:, n_samp:n_samp + 1], (lanes, lanes))

    @pl.loop(0, half - 1)
    def _(t):
        source = lax.rem(high + half - 1 - t, half)
        line_copy(t, source, high).wait_recv()
        out_ref[...] += line_in[source].astype(jnp.float32)

    out_ref[...] *= scale[...]

    to_sibling(feat).wait_send()
    for offset in range(1, chips):
        @pl.loop(0, chunks)
        def _(k):
            cross(offset, k, feat, far(offset)).wait_send()
            relay(offset, k, far(chips - offset)).wait_send()

    @pl.loop(0, half)
    def _(t):
        near_copy(t).wait_send()

        @pl.when(t < half - 1)
        def _():
            line_copy(t, high, lax.rem(high + 1 + t, half)).wait_send()

    @pl.loop(1, n_samp)
    def _(t):
        stats_copy(lax.rem(samp + t, n_samp), samp).wait_send()


def per_device(n_feat, n_samp, tier_one, residuals, pair_list):
    rows, samples = tier_one.shape
    pairs = pair_list.shape[1]
    chips = n_feat // 2
    owned = pairs // n_samp
    sub = min(owned // 2, 128)
    chunks = 8
    sizes = (n_feat, n_samp, rows, samples, pairs, chunks)
    dma = pltpu.SemaphoreType.DMA
    return pl.pallas_call(
        functools.partial(kernel, sizes),
        out_shape=jax.ShapeDtypeStruct((owned, lanes), jnp.float32),
        in_specs=[
            pl.BlockSpec(memory_space=pl.ANY),
            pl.BlockSpec(memory_space=pltpu.VMEM),
            pl.BlockSpec(memory_space=pltpu.SMEM),
            pl.BlockSpec(memory_space=pltpu.VMEM),
        ],
        out_specs=pl.BlockSpec(memory_space=pltpu.VMEM),
        scratch_shapes=[
            pltpu.VMEM((n_feat, rows, samples), jnp.bfloat16),
            pltpu.VMEM((n_feat * rows, 4, lanes), jnp.float32),
            pltpu.VMEM((sub * 4, lanes), jnp.float32),
            pltpu.VMEM((sub * 4, lanes), jnp.float32),
            pltpu.VMEM((sub * 4, lanes), jnp.float32),
            pltpu.VMEM((sub * 4, lanes), jnp.float32),
            pltpu.VMEM((pairs, lanes), jnp.int32),
            pltpu.VMEM((samples, 2 * lanes), jnp.bfloat16),
            pltpu.VMEM((owned, lanes), jnp.float32),
            pltpu.VMEM((owned, lanes), jnp.float32),
            pltpu.VMEM((n_samp // 2, owned, lanes), jnp.bfloat16),
            pltpu.VMEM((n_samp // 2, owned, lanes), jnp.bfloat16),
            pltpu.VMEM((n_samp // 2, owned, lanes), jnp.bfloat16),
            pltpu.VMEM((n_samp // 2, owned, lanes), jnp.bfloat16),
            pltpu.VMEM((n_samp, 4, owned), jnp.float32),
            pltpu.VMEM((n_samp, 4, owned), jnp.float32),
            pltpu.VMEM((lanes, owned), jnp.float32),
            pltpu.VMEM((owned, lanes), jnp.float32),
            dma,
            dma((max(chips - 1, 1), chunks)),
            dma((max(chips - 1, 1), chunks)),
            dma,
            dma,
            dma((max(chips - 1, 1), chunks)),
            dma((max(chips - 1, 1), chunks)),
            dma((n_samp // 2,)),
            dma((n_samp // 2,)),
            dma((n_samp // 2,)),
            dma((n_samp // 2,)),
            dma((n_samp,)),
            dma((n_samp,)),
        ],
        compiler_params=pltpu.CompilerParams(
            collective_id=0, has_side_effects=True, vmem_limit_bytes=56 * 2**20
        ),
    )(tier_one, residuals, pair_list[:2].reshape(2 * pairs), pair_list)


def solution(mesh):
    in_specs = (P("feat", "samp"), P("samp", None), P(None, "feat"))
    out_specs = P(("feat", "samp"), None)
    return jax.shard_map(
        functools.partial(per_device, mesh.shape["feat"], mesh.shape["samp"]),
        mesh=mesh, in_specs=in_specs, out_specs=out_specs, check_vma=False,
    )
```

```python
import functools
import math

import jax
import jax.numpy as jnp
from jax import lax
from jax.experimental import pallas as pl
from jax.experimental.pallas import tpu as pltpu
from jax.sharding import PartitionSpec as P

epsilon = 1e-05
MESH = pl.DeviceIdType.MESH
lanes = 128


def kernel(
    sizes, tier_ref, res_any, pair_any, out_ref,
    res_ref, pair_smem, pair_vmem, slots, table, first_even, second_even, first_odd, second_odd,
    op_wide, weights, share_block, stats_wide,
    near_out, near_in, line_out, line_in, send_stats, recv_stats, turned, scale,
    own_sem, small_sems, cross_send, cross_recv, sib_send, sib_recv, relay_send, relay_recv,
    near_send, near_recv, line_send, line_recv, stats_send, stats_recv,
):
    n_feat, n_samp, rows, samples, pairs, chunks = sizes
    chips = n_feat // 2
    pieces = samples // lanes
    owned = pairs // n_samp
    sub = min(owned // 2, 128)
    group, tall = 8, 16
    step = rows // chunks
    total_samples = samples * n_samp
    feat = lax.axis_index("feat")
    samp = lax.axis_index("samp")
    chip = feat // 2
    core = lax.rem(feat, 2)
    sibling = chip * 2 + 1 - core
    half = n_samp // 2
    high = samp // 2
    low = lax.rem(samp, 2)
    partner = high * 2 + 1 - low

    def far(offset):
        return lax.rem(chip + offset, chips) * 2 + core

    barrier = pltpu.get_barrier_semaphore()
    pl.semaphore_signal(barrier, inc=1, device_id=(sibling, samp), device_id_type=MESH)
    for offset in range(1, chips):
        pl.semaphore_signal(barrier, inc=1, device_id=(far(offset), samp), device_id_type=MESH)
    for offset in range(1, n_samp):
        pl.semaphore_signal(
            barrier, inc=1, device_id=(feat, lax.rem(samp + offset, n_samp)), device_id_type=MESH
        )
    own_copy = pltpu.make_async_copy(tier_ref, slots.at[feat], own_sem)
    own_copy.start()
    pl.semaphore_wait(barrier, 1 + (chips - 1) + (n_samp - 1))

    def part(index):
        return pl.ds(pl.multiple_of(index * step, step), step)

    def cross(offset, k, holder, target):
        return pltpu.make_async_remote_copy(
            src_ref=tier_ref.at[part(k)],
            dst_ref=slots.at[holder, part(k)],
            send_sem=cross_send.at[offset - 1, k],
            recv_sem=cross_recv.at[offset - 1, k],
            device_id=(target, samp),
            device_id_type=MESH,
        )

    def relay(offset, k, holder):
        return pltpu.make_async_remote_copy(
            src_ref=slots.at[holder, part(k)],
            dst_ref=slots.at[holder, part(k)],
            send_sem=relay_send.at[offset - 1, k],
            recv_sem=relay_recv.at[offset - 1, k],
            device_id=(sibling, samp),
            device_id_type=MESH,
        )

    def to_sibling(holder):
        return pltpu.make_async_remote_copy(
            src_ref=tier_ref,
            dst_ref=slots.at[holder],
            send_sem=sib_send,
            recv_sem=sib_recv,
            device_id=(sibling, samp),
            device_id_type=MESH,
        )

    for offset in range(1, chips):
        @pl.loop(0, chunks)
        def _(k):
            cross(offset, k, feat, far(offset)).start()
    to_sibling(feat).start()

    flat = table.reshape(n_feat * rows * 4, lanes)

    def widen(holder, k):
        @pl.loop(0, step // 64 if step % 64 == 0 else 1)
        def _(g):
            size = 64 if step % 64 == 0 else step
            start = pl.multiple_of(k * step + g * size, size)
            for j in range(pieces):
                values = slots[holder, pl.ds(start, size), j * lanes:(j + 1) * lanes]
                flat[pl.ds(4 * (holder * rows + start) + j, size, stride=4), :] = values.astype(jnp.float32)

    small_copies = [
        pltpu.make_async_copy(pair_any, pair_vmem, small_sems.at[0]),
        pltpu.make_async_copy(res_any, res_ref, small_sems.at[1]),
        pltpu.make_async_copy(pair_any, pair_smem, small_sems.at[2]),
    ]
    for copy in small_copies:
        copy.start()
    for copy in small_copies:
        copy.wait()

    weights[:, :lanes] = res_ref[...]
    weights[:, lanes:] = jnp.ones((samples, lanes), jnp.bfloat16)
    col_local = jnp.sum(res_ref[...].astype(jnp.float32), axis=0, keepdims=True)

    @pl.loop(0, pairs // lanes)
    def _(g):
        span = pl.ds(pl.multiple_of(g * lanes, lanes), lanes)
        op_wide[span, :] = jnp.broadcast_to(pair_vmem[g, 2:3, :], (lanes, lanes)).T

    own_copy.wait()

    @pl.loop(0, chunks)
    def _(k):
        widen(feat, k)

    to_sibling(sibling).wait_recv()

    @pl.loop(0, chunks)
    def _(k):
        widen(sibling, k)

    for offset in range(1, chips):
        mine = far(chips - offset)
        theirs = mine + 1 - 2 * core

        @pl.loop(0, chunks)
        def _(k):
            cross(offset, k, mine, feat).wait_recv()
            relay(offset, k, mine).start()
            widen(mine, k)

            @pl.when(k > 0)
            def _():
                relay(offset, k - 1, theirs).wait_recv()
                widen(theirs, k - 1)

        relay(offset, chunks - 1, theirs).wait_recv()
        widen(theirs, chunks - 1)

    lane_id = lax.broadcasted_iota(jnp.int32, (sub, lanes), 1)

    def owner_of(b):
        return lax.rem(high + 1 + b, half) * 2 + lax.rem(low + 1 + b // half, 2)

    def index_of(which, base, p):
        inside = 0 if sub % lanes == 0 else lax.rem(base, lanes)
        return pair_smem[base // lanes, which, inside + p]

    def gather(stages, base, p):
        firsts = [table[index_of(0, base, p + u)] for u in range(group)]
        seconds = [table[index_of(1, base, p + u)] for u in range(group)]
        for u in range(group):
            stages[0][4 * (p + u):4 * (p + u) + 4, :] = firsts[u]
            stages[1][4 * (p + u):4 * (p + u) + 4, :] = seconds[u]

    def build(stages, base, p):
        op = op_wide[pl.ds(pl.multiple_of(base + p, tall), tall), :]
        parts = []
        square = jnp.zeros((tall, lanes), jnp.float32)
        for j in range(pieces):
            a = stages[0][pl.ds(4 * p + j, tall, stride=4), :]
            b = stages[1][pl.ds(4 * p + j, tall, stride=4), :]
            plain = a + jnp.where(op == 1, -b, b)
            other = jnp.where(op == 2, a * b, a / (1.0 + jnp.abs(b)))
            built = jnp.where(op < 2, plain, other).astype(jnp.bfloat16)
            parts.append(built)
            wide = built.astype(jnp.float32)
            square += wide * wide
        return jnp.concatenate(parts, axis=1), jnp.sum(square, axis=1, keepdims=True)

    def advance(now, base, later, next_base, here):
        built, squares = [], []
        steps = sub // tall
        share = sub // 2 // steps
        for i in range(steps):
            one, square = build(now, base, i * tall)
            built.append(one)
            squares.append(square)
            for p in range(i * share, (i + 1) * share, group):
                gather(later, next_base, p)
        both = jnp.dot(
            jnp.concatenate(built, axis=0), weights[...], preferred_element_type=jnp.float32
        )
        for p in range(sub // 2, sub, group):
            gather(later, next_base, p)
        sums = both[:, lanes:]
        share_block[here, :] = both[:, :lanes] - sums * (col_local / samples)
        stats_wide[here, :] = jnp.where(lane_id == 0, sums, jnp.concatenate(squares, axis=0))

    even = (first_even, second_even)
    odd = (first_odd, second_odd)

    @pl.loop(0, sub // group)
    def _(g):
        base = owner_of(0) * owned
        firsts = [table[index_of(0, base, g * group + u)] for u in range(group)]
        seconds = [table[index_of(1, base, g * group + u)] for u in range(group)]
        for u in range(group):
            spot = pl.ds(pl.multiple_of((g * group + u) * 4, 4), 4)
            first_even[spot, :] = firsts[u]
            second_even[spot, :] = seconds[u]

    couples = owned // (2 * sub)

    def make_block(b, owner):
        @pl.loop(0, couples)
        def _(h):
            base = owner * owned + h * (2 * sub)
            after = b * couples + h + 1
            next_base = owner_of(after // couples) * owned + lax.rem(after, couples) * (2 * sub)
            first_half = pl.ds(pl.multiple_of(h * (2 * sub), sub), sub)
            second_half = pl.ds(pl.multiple_of(h * (2 * sub) + sub, sub), sub)
            advance(even, base, odd, base + sub, first_half)
            advance(odd, base + sub, even, next_base, second_half)

        for q in range(owned // lanes):
            flipped = stats_wide[q * lanes:(q + 1) * lanes, :].T
            send_stats[owner, 0:2, q * lanes:(q + 1) * lanes] = flipped[0:2, :]
        send_stats[owner, 2:3, 0:lanes] = col_local

    def near_copy(t):
        return pltpu.make_async_remote_copy(
            src_ref=near_out.at[t],
            dst_ref=near_in.at[t],
            send_sem=near_send.at[t],
            recv_sem=near_recv.at[t],
            device_id=(feat, partner),
            device_id_type=MESH,
        )

    def line_copy(t, source, target):
        return pltpu.make_async_remote_copy(
            src_ref=line_out.at[t],
            dst_ref=line_in.at[source],
            send_sem=line_send.at[t],
            recv_sem=line_recv.at[source],
            device_id=(feat, target * 2 + low),
            device_id_type=MESH,
        )

    def stats_copy(owner, source):
        return pltpu.make_async_remote_copy(
            src_ref=send_stats.at[owner],
            dst_ref=recv_stats.at[source],
            send_sem=stats_send.at[owner],
            recv_sem=stats_recv.at[source],
            device_id=(feat, owner),
            device_id_type=MESH,
        )

    @pl.loop(0, n_samp)
    def _(b):
        owner = owner_of(b)
        make_block(b, owner)

        @pl.when(b < half)
        def _():
            near_out[b] = share_block[...].astype(jnp.bfloat16)
            near_copy(b).start()
            stats_copy(owner, samp).start()

        @pl.when(b >= half)
        def _():
            t = b - half
            near_copy(t).wait_recv()
            total = share_block[...] + near_in[t].astype(jnp.float32)
            line_out[t] = total.astype(jnp.bfloat16)
            out_ref[...] = total

            @pl.when(t < half - 1)
            def _():
                line_copy(t, high, lax.rem(high + 1 + t, half)).start()
                stats_copy(owner, samp).start()

    recv_stats[samp] = send_stats[samp]

    @pl.loop(1, n_samp)
    def _(t):
        stats_copy(samp, lax.rem(samp + n_samp - t, n_samp)).wait_recv()

    first_sums = jnp.zeros((1, owned), jnp.float32)
    square_sums = jnp.zeros((1, owned), jnp.float32)
    for d in range(n_samp):
        first_sums += recv_stats[d, 0:1, :]
        square_sums += recv_stats[d, 1:2, :]
    means = first_sums / total_samples
    variance = square_sums / total_samples - means * means
    turned[n_samp:n_samp + 1, :] = lax.rsqrt(variance + epsilon) / math.sqrt(total_samples)
    for d in range(n_samp):
        turned[d:d + 1, :] = recv_stats[d, 0:1, :] / samples - means

    @pl.loop(0, owned // lanes)
    def _(q):
        span = pl.ds(pl.multiple_of(q * lanes, lanes), lanes)
        columns = turned[:, span].T
        total = out_ref[span, :]
        for d in range(n_samp):
            total += columns[:, d:d + 1] * recv_stats[d, 2:3, 0:lanes]
        out_ref[span, :] = total
        scale[span, :] = jnp.broadcast_to(columns[:, n_samp:n_samp + 1], (lanes, lanes))

    @pl.loop(0, half - 1)
    def _(t):
        source = lax.rem(high + half - 1 - t, half)
        line_copy(t, source, high).wait_recv()
        out_ref[...] += line_in[source].astype(jnp.float32)

    out_ref[...] *= scale[...]

    to_sibling(feat).wait_send()
    for offset in range(1, chips):
        @pl.loop(0, chunks)
        def _(k):
            cross(offset, k, feat, far(offset)).wait_send()
            relay(offset, k, far(chips - offset)).wait_send()

    @pl.loop(0, half)
    def _(t):
        near_copy(t).wait_send()

        @pl.when(t < half - 1)
        def _():
            line_copy(t, high, lax.rem(high + 1 + t, half)).wait_send()

    @pl.loop(1, n_samp)
    def _(t):
        stats_copy(lax.rem(samp + t, n_samp), samp).wait_send()


def per_device(n_feat, n_samp, tier_one, residuals, pair_list):
    rows, samples = tier_one.shape
    pairs = pair_list.shape[1]
    chips = n_feat // 2
    owned = pairs // n_samp
    sub = min(owned // 2, 128)
    chunks = 8
    sizes = (n_feat, n_samp, rows, samples, pairs, chunks)
    dma = pltpu.SemaphoreType.DMA
    tiled = pair_list.reshape(3, pairs // lanes, lanes).transpose(1, 0, 2)
    return pl.pallas_call(
        functools.partial(kernel, sizes),
        out_shape=jax.ShapeDtypeStruct((owned, lanes), jnp.float32),
        in_specs=[
            pl.BlockSpec(memory_space=pl.ANY),
            pl.BlockSpec(memory_space=pl.ANY),
            pl.BlockSpec(memory_space=pl.ANY),
        ],
        out_specs=pl.BlockSpec(memory_space=pltpu.VMEM),
        scratch_shapes=[
            pltpu.VMEM((samples, lanes), jnp.bfloat16),
            pltpu.SMEM((pairs // lanes, 3, lanes), jnp.int32),
            pltpu.VMEM((pairs // lanes, 3, lanes), jnp.int32),
            pltpu.VMEM((n_feat, rows, samples), jnp.bfloat16),
            pltpu.VMEM((n_feat * rows, 4, lanes), jnp.float32),
            pltpu.VMEM((sub * 4, lanes), jnp.float32),
            pltpu.VMEM((sub * 4, lanes), jnp.float32),
            pltpu.VMEM((sub * 4, lanes), jnp.float32),
            pltpu.VMEM((sub * 4, lanes), jnp.float32),
            pltpu.VMEM((pairs, lanes), jnp.int32),
            pltpu.VMEM((samples, 2 * lanes), jnp.bfloat16),
            pltpu.VMEM((owned, lanes), jnp.float32),
            pltpu.VMEM((owned, lanes), jnp.float32),
            pltpu.VMEM((n_samp // 2, owned, lanes), jnp.bfloat16),
            pltpu.VMEM((n_samp // 2, owned, lanes), jnp.bfloat16),
            pltpu.VMEM((n_samp // 2, owned, lanes), jnp.bfloat16),
            pltpu.VMEM((n_samp // 2, owned, lanes), jnp.bfloat16),
            pltpu.VMEM((n_samp, 4, owned), jnp.float32),
            pltpu.VMEM((n_samp, 4, owned), jnp.float32),
            pltpu.VMEM((lanes, owned), jnp.float32),
            pltpu.VMEM((owned, lanes), jnp.float32),
            dma,
            dma((3,)),
            dma((max(chips - 1, 1), chunks)),
            dma((max(chips - 1, 1), chunks)),
            dma,
            dma,
            dma((max(chips - 1, 1), chunks)),
            dma((max(chips - 1, 1), chunks)),
            dma((n_samp // 2,)),
            dma((n_samp // 2,)),
            dma((n_samp // 2,)),
            dma((n_samp // 2,)),
            dma((n_samp,)),
            dma((n_samp,)),
        ],
        compiler_params=pltpu.CompilerParams(
            collective_id=0, has_side_effects=True, vmem_limit_bytes=56 * 2**20
        ),
    )(tier_one, residuals, tiled)


def solution(mesh):
    in_specs = (P("feat", "samp"), P("samp", None), P(None, "feat"))
    out_specs = P(("feat", "samp"), None)
    return jax.shard_map(
        functools.partial(per_device, mesh.shape["feat"], mesh.shape["samp"]),
        mesh=mesh, in_specs=in_specs, out_specs=out_specs, check_vma=False,
    )
```

```python
import functools
import math

import jax
import jax.numpy as jnp
from jax import lax
from jax.experimental import pallas as pl
from jax.experimental.pallas import tpu as pltpu
from jax.sharding import PartitionSpec as P

epsilon = 1e-05
MESH = pl.DeviceIdType.MESH
lanes = 128


def kernel(
    sizes, tier_ref, res_any, pair_any, out_ref,
    res_ref, pair_smem, pair_vmem, slots, table, first_even, second_even, first_odd, second_odd,
    op_wide, weights, share_block, stats_wide,
    near_out, near_in, line_out, line_in, send_stats, recv_stats, turned, scale,
    own_sem, small_sems, cross_send, cross_recv, sib_send, sib_recv, relay_send, relay_recv,
    near_send, near_recv, line_send, line_recv, stats_send, stats_recv,
):
    n_feat, n_samp, rows, samples, pairs, chunks = sizes
    chips = n_feat // 2
    pieces = samples // lanes
    owned = pairs // n_samp
    sub = min(owned // 2, 128)
    group, tall = 8, 16
    step = rows // chunks
    total_samples = samples * n_samp
    feat = lax.axis_index("feat")
    samp = lax.axis_index("samp")
    chip = feat // 2
    core = lax.rem(feat, 2)
    sibling = chip * 2 + 1 - core
    half = n_samp // 2
    high = samp // 2
    low = lax.rem(samp, 2)
    partner = high * 2 + 1 - low

    def far(offset):
        return lax.rem(chip + offset, chips) * 2 + core

    barrier = pltpu.get_barrier_semaphore()
    pl.semaphore_signal(barrier, inc=1, device_id=(sibling, samp), device_id_type=MESH)
    for offset in range(1, chips):
        pl.semaphore_signal(barrier, inc=1, device_id=(far(offset), samp), device_id_type=MESH)
    for offset in range(1, n_samp):
        pl.semaphore_signal(
            barrier, inc=1, device_id=(feat, lax.rem(samp + offset, n_samp)), device_id_type=MESH
        )
    own_copy = pltpu.make_async_copy(tier_ref, slots.at[feat], own_sem)
    own_copy.start()
    pl.semaphore_wait(barrier, 1 + (chips - 1) + (n_samp - 1))

    def part(index):
        return pl.ds(pl.multiple_of(index * step, step), step)

    def cross(offset, k, holder, target):
        return pltpu.make_async_remote_copy(
            src_ref=tier_ref.at[part(k)],
            dst_ref=slots.at[holder, part(k)],
            send_sem=cross_send.at[offset - 1, k],
            recv_sem=cross_recv.at[offset - 1, k],
            device_id=(target, samp),
            device_id_type=MESH,
        )

    def relay(offset, k, holder):
        return pltpu.make_async_remote_copy(
            src_ref=slots.at[holder, part(k)],
            dst_ref=slots.at[holder, part(k)],
            send_sem=relay_send.at[offset - 1, k],
            recv_sem=relay_recv.at[offset - 1, k],
            device_id=(sibling, samp),
            device_id_type=MESH,
        )

    def to_sibling(holder):
        return pltpu.make_async_remote_copy(
            src_ref=tier_ref,
            dst_ref=slots.at[holder],
            send_sem=sib_send,
            recv_sem=sib_recv,
            device_id=(sibling, samp),
            device_id_type=MESH,
        )

    for offset in range(1, chips):
        @pl.loop(0, chunks)
        def _(k):
            cross(offset, k, feat, far(offset)).start()
    to_sibling(feat).start()

    flat = table.reshape(n_feat * rows * 4, lanes)

    def widen(holder, k):
        @pl.loop(0, step // 64 if step % 64 == 0 else 1)
        def _(g):
            size = 64 if step % 64 == 0 else step
            start = pl.multiple_of(k * step + g * size, size)
            for j in range(pieces):
                values = slots[holder, pl.ds(start, size), j * lanes:(j + 1) * lanes]
                flat[pl.ds(4 * (holder * rows + start) + j, size, stride=4), :] = values.astype(jnp.float32)

    small_copies = [
        pltpu.make_async_copy(pair_any, pair_vmem, small_sems.at[0]),
        pltpu.make_async_copy(res_any, res_ref, small_sems.at[1]),
        pltpu.make_async_copy(pair_any, pair_smem, small_sems.at[2]),
    ]
    for copy in small_copies:
        copy.start()
    for copy in small_copies:
        copy.wait()

    weights[:, :lanes] = res_ref[...]
    weights[:, lanes:] = jnp.ones((samples, lanes), jnp.bfloat16)
    col_local = jnp.sum(res_ref[...].astype(jnp.float32), axis=0, keepdims=True)

    @pl.loop(0, pairs // lanes)
    def _(g):
        span = pl.ds(pl.multiple_of(g * lanes, lanes), lanes)
        op_wide[span, :] = jnp.broadcast_to(pair_vmem[g, 2:3, :], (lanes, lanes)).T

    own_copy.wait()

    @pl.loop(0, chunks)
    def _(k):
        widen(feat, k)

    to_sibling(sibling).wait_recv()

    @pl.loop(0, chunks)
    def _(k):
        widen(sibling, k)

    for offset in range(1, chips):
        mine = far(chips - offset)
        theirs = mine + 1 - 2 * core

        @pl.loop(0, chunks)
        def _(k):
            cross(offset, k, mine, feat).wait_recv()
            relay(offset, k, mine).start()
            widen(mine, k)

            @pl.when(k > 0)
            def _():
                relay(offset, k - 1, theirs).wait_recv()
                widen(theirs, k - 1)

        relay(offset, chunks - 1, theirs).wait_recv()
        widen(theirs, chunks - 1)

    lane_id = lax.broadcasted_iota(jnp.int32, (sub, lanes), 1)

    def owner_of(b):
        return lax.rem(high + 1 + b, half) * 2 + lax.rem(low + 1 + b // half, 2)

    def index_of(which, base, p):
        inside = 0 if sub % lanes == 0 else lax.rem(base, lanes)
        return pair_smem[base // lanes, which, inside + p]

    def fetch(base, p):
        return (
            [table[index_of(0, base, p + u)] for u in range(group)],
            [table[index_of(1, base, p + u)] for u in range(group)],
        )

    def stage(stages, p, fetched):
        for u in range(group):
            stages[0][4 * (p + u):4 * (p + u) + 4, :] = fetched[0][u]
            stages[1][4 * (p + u):4 * (p + u) + 4, :] = fetched[1][u]

    def build(stages, base, p):
        op = op_wide[pl.ds(pl.multiple_of(base + p, tall), tall), :]
        parts = []
        square = jnp.zeros((tall, lanes), jnp.float32)
        for j in range(pieces):
            a = stages[0][pl.ds(4 * p + j, tall, stride=4), :]
            b = stages[1][pl.ds(4 * p + j, tall, stride=4), :]
            plain = a + jnp.where(op == 1, -b, b)
            other = jnp.where(op == 2, a * b, a / (1.0 + jnp.abs(b)))
            built = jnp.where(op < 2, plain, other).astype(jnp.bfloat16)
            parts.append(built)
            wide = built.astype(jnp.float32)
            square += wide * wide
        return jnp.concatenate(parts, axis=1), jnp.sum(square, axis=1, keepdims=True)

    def advance(now, base, later, next_base, here):
        built, squares = [], []
        steps = sub // tall
        share = sub // 2 // steps
        fetched = fetch(next_base, 0)
        for i in range(steps):
            one, square = build(now, base, i * tall)
            built.append(one)
            squares.append(square)
            for p in range(i * share, (i + 1) * share, group):
                following = fetch(next_base, p + group)
                stage(later, p, fetched)
                fetched = following
        both = jnp.dot(
            jnp.concatenate(built, axis=0), weights[...], preferred_element_type=jnp.float32
        )
        for p in range(sub // 2, sub, group):
            following = fetch(next_base, p + group) if p + group < sub else None
            stage(later, p, fetched)
            fetched = following
        sums = both[:, lanes:]
        share_block[here, :] = both[:, :lanes] - sums * (col_local / samples)
        stats_wide[here, :] = jnp.where(lane_id == 0, sums, jnp.concatenate(squares, axis=0))

    even = (first_even, second_even)
    odd = (first_odd, second_odd)

    @pl.loop(0, sub // group)
    def _(g):
        base = owner_of(0) * owned
        firsts = [table[index_of(0, base, g * group + u)] for u in range(group)]
        seconds = [table[index_of(1, base, g * group + u)] for u in range(group)]
        for u in range(group):
            spot = pl.ds(pl.multiple_of((g * group + u) * 4, 4), 4)
            first_even[spot, :] = firsts[u]
            second_even[spot, :] = seconds[u]

    couples = owned // (2 * sub)

    def make_block(b, owner):
        @pl.loop(0, couples)
        def _(h):
            base = owner * owned + h * (2 * sub)
            after = b * couples + h + 1
            next_base = owner_of(after // couples) * owned + lax.rem(after, couples) * (2 * sub)
            first_half = pl.ds(pl.multiple_of(h * (2 * sub), sub), sub)
            second_half = pl.ds(pl.multiple_of(h * (2 * sub) + sub, sub), sub)
            advance(even, base, odd, base + sub, first_half)
            advance(odd, base + sub, even, next_base, second_half)

        for q in range(owned // lanes):
            flipped = stats_wide[q * lanes:(q + 1) * lanes, :].T
            send_stats[owner, 0:2, q * lanes:(q + 1) * lanes] = flipped[0:2, :]
        send_stats[owner, 2:3, 0:lanes] = col_local

    def near_copy(t):
        return pltpu.make_async_remote_copy(
            src_ref=near_out.at[t],
            dst_ref=near_in.at[t],
            send_sem=near_send.at[t],
            recv_sem=near_recv.at[t],
            device_id=(feat, partner),
            device_id_type=MESH,
        )

    def line_copy(t, source, target):
        return pltpu.make_async_remote_copy(
            src_ref=line_out.at[t],
            dst_ref=line_in.at[source],
            send_sem=line_send.at[t],
            recv_sem=line_recv.at[source],
            device_id=(feat, target * 2 + low),
            device_id_type=MESH,
        )

    def stats_copy(owner, source):
        return pltpu.make_async_remote_copy(
            src_ref=send_stats.at[owner],
            dst_ref=recv_stats.at[source],
            send_sem=stats_send.at[owner],
            recv_sem=stats_recv.at[source],
            device_id=(feat, owner),
            device_id_type=MESH,
        )

    @pl.loop(0, n_samp)
    def _(b):
        owner = owner_of(b)
        make_block(b, owner)

        @pl.when(b < half)
        def _():
            near_out[b] = share_block[...].astype(jnp.bfloat16)
            near_copy(b).start()
            stats_copy(owner, samp).start()

        @pl.when(b >= half)
        def _():
            t = b - half
            near_copy(t).wait_recv()
            total = share_block[...] + near_in[t].astype(jnp.float32)
            line_out[t] = total.astype(jnp.bfloat16)
            out_ref[...] = total

            @pl.when(t < half - 1)
            def _():
                line_copy(t, high, lax.rem(high + 1 + t, half)).start()
                stats_copy(owner, samp).start()

    recv_stats[samp] = send_stats[samp]

    @pl.loop(1, n_samp)
    def _(t):
        stats_copy(samp, lax.rem(samp + n_samp - t, n_samp)).wait_recv()

    first_sums = jnp.zeros((1, owned), jnp.float32)
    square_sums = jnp.zeros((1, owned), jnp.float32)
    for d in range(n_samp):
        first_sums += recv_stats[d, 0:1, :]
        square_sums += recv_stats[d, 1:2, :]
    means = first_sums / total_samples
    variance = square_sums / total_samples - means * means
    turned[n_samp:n_samp + 1, :] = lax.rsqrt(variance + epsilon) / math.sqrt(total_samples)
    for d in range(n_samp):
        turned[d:d + 1, :] = recv_stats[d, 0:1, :] / samples - means

    @pl.loop(0, owned // lanes)
    def _(q):
        span = pl.ds(pl.multiple_of(q * lanes, lanes), lanes)
        columns = turned[:, span].T
        total = out_ref[span, :]
        for d in range(n_samp):
            total += columns[:, d:d + 1] * recv_stats[d, 2:3, 0:lanes]
        out_ref[span, :] = total
        scale[span, :] = jnp.broadcast_to(columns[:, n_samp:n_samp + 1], (lanes, lanes))

    @pl.loop(0, half - 1)
    def _(t):
        source = lax.rem(high + half - 1 - t, half)
        line_copy(t, source, high).wait_recv()
        out_ref[...] += line_in[source].astype(jnp.float32)

    out_ref[...] *= scale[...]

    to_sibling(feat).wait_send()
    for offset in range(1, chips):
        @pl.loop(0, chunks)
        def _(k):
            cross(offset, k, feat, far(offset)).wait_send()
            relay(offset, k, far(chips - offset)).wait_send()

    @pl.loop(0, half)
    def _(t):
        near_copy(t).wait_send()

        @pl.when(t < half - 1)
        def _():
            line_copy(t, high, lax.rem(high + 1 + t, half)).wait_send()

    @pl.loop(1, n_samp)
    def _(t):
        stats_copy(lax.rem(samp + t, n_samp), samp).wait_send()


def per_device(n_feat, n_samp, tier_one, residuals, pair_list):
    rows, samples = tier_one.shape
    pairs = pair_list.shape[1]
    chips = n_feat // 2
    owned = pairs // n_samp
    sub = min(owned // 2, 128)
    chunks = 16
    sizes = (n_feat, n_samp, rows, samples, pairs, chunks)
    dma = pltpu.SemaphoreType.DMA
    tiled = pair_list.reshape(3, pairs // lanes, lanes).transpose(1, 0, 2)
    return pl.pallas_call(
        functools.partial(kernel, sizes),
        out_shape=jax.ShapeDtypeStruct((owned, lanes), jnp.float32),
        in_specs=[
            pl.BlockSpec(memory_space=pl.ANY),
            pl.BlockSpec(memory_space=pl.ANY),
            pl.BlockSpec(memory_space=pl.ANY),
        ],
        out_specs=pl.BlockSpec(memory_space=pltpu.VMEM),
        scratch_shapes=[
            pltpu.VMEM((samples, lanes), jnp.bfloat16),
            pltpu.SMEM((pairs // lanes, 3, lanes), jnp.int32),
            pltpu.VMEM((pairs // lanes, 3, lanes), jnp.int32),
            pltpu.VMEM((n_feat, rows, samples), jnp.bfloat16),
            pltpu.VMEM((n_feat * rows, 4, lanes), jnp.float32),
            pltpu.VMEM((sub * 4, lanes), jnp.float32),
            pltpu.VMEM((sub * 4, lanes), jnp.float32),
            pltpu.VMEM((sub * 4, lanes), jnp.float32),
            pltpu.VMEM((sub * 4, lanes), jnp.float32),
            pltpu.VMEM((pairs, lanes), jnp.int32),
            pltpu.VMEM((samples, 2 * lanes), jnp.bfloat16),
            pltpu.VMEM((owned, lanes), jnp.float32),
            pltpu.VMEM((owned, lanes), jnp.float32),
            pltpu.VMEM((n_samp // 2, owned, lanes), jnp.bfloat16),
            pltpu.VMEM((n_samp // 2, owned, lanes), jnp.bfloat16),
            pltpu.VMEM((n_samp // 2, owned, lanes), jnp.bfloat16),
            pltpu.VMEM((n_samp // 2, owned, lanes), jnp.bfloat16),
            pltpu.VMEM((n_samp, 4, owned), jnp.float32),
            pltpu.VMEM((n_samp, 4, owned), jnp.float32),
            pltpu.VMEM((lanes, owned), jnp.float32),
            pltpu.VMEM((owned, lanes), jnp.float32),
            dma,
            dma((3,)),
            dma((max(chips - 1, 1), chunks)),
            dma((max(chips - 1, 1), chunks)),
            dma,
            dma,
            dma((max(chips - 1, 1), chunks)),
            dma((max(chips - 1, 1), chunks)),
            dma((n_samp // 2,)),
            dma((n_samp // 2,)),
            dma((n_samp // 2,)),
            dma((n_samp // 2,)),
            dma((n_samp,)),
            dma((n_samp,)),
        ],
        compiler_params=pltpu.CompilerParams(
            collective_id=0, has_side_effects=True, vmem_limit_bytes=56 * 2**20
        ),
    )(tier_one, residuals, tiled)


def solution(mesh):
    in_specs = (P("feat", "samp"), P("samp", None), P(None, "feat"))
    out_specs = P(("feat", "samp"), None)
    return jax.shard_map(
        functools.partial(per_device, mesh.shape["feat"], mesh.shape["samp"]),
        mesh=mesh, in_specs=in_specs, out_specs=out_specs, check_vma=False,
    )
```

```python
import functools
import math

import jax
import jax.numpy as jnp
from jax import lax
from jax.experimental import pallas as pl
from jax.experimental.pallas import tpu as pltpu
from jax.sharding import PartitionSpec as P

epsilon = 1e-05
MESH = pl.DeviceIdType.MESH
lanes = 128


def kernel(
    sizes, tier_ref, res_any, pair_any, out_ref,
    res_ref, pair_smem, pair_vmem, slots, table, first_even, second_even, first_odd, second_odd,
    op_wide, weights, share_block, stats_wide,
    near_out, near_in, line_out, line_in, send_stats, recv_stats, turned, scale,
    own_sem, small_sems, cross_send, cross_recv, sib_send, sib_recv, relay_send, relay_recv,
    near_send, near_recv, line_send, line_recv, stats_send, stats_recv,
):
    n_feat, n_samp, rows, samples, pairs, chunks = sizes
    chips = n_feat // 2
    pieces = samples // lanes
    owned = pairs // n_samp
    sub = min(owned // 2, 128)
    group, tall = 8, 16
    step = rows // chunks
    total_samples = samples * n_samp
    feat = lax.axis_index("feat")
    samp = lax.axis_index("samp")
    chip = feat // 2
    core = lax.rem(feat, 2)
    sibling = chip * 2 + 1 - core
    half = n_samp // 2
    high = samp // 2
    low = lax.rem(samp, 2)
    partner = high * 2 + 1 - low

    def far(offset):
        return lax.rem(chip + offset, chips) * 2 + core

    barrier = pltpu.get_barrier_semaphore()
    pl.semaphore_signal(barrier, inc=1, device_id=(sibling, samp), device_id_type=MESH)
    for offset in range(1, chips):
        pl.semaphore_signal(barrier, inc=1, device_id=(far(offset), samp), device_id_type=MESH)
    for offset in range(1, n_samp):
        pl.semaphore_signal(
            barrier, inc=1, device_id=(feat, lax.rem(samp + offset, n_samp)), device_id_type=MESH
        )
    own_copy = pltpu.make_async_copy(tier_ref, slots.at[feat], own_sem)
    own_copy.start()
    pl.semaphore_wait(barrier, 1 + (chips - 1) + (n_samp - 1))

    def part(index):
        return pl.ds(pl.multiple_of(index * step, step), step)

    def cross(offset, k, holder, target):
        return pltpu.make_async_remote_copy(
            src_ref=tier_ref.at[part(k)],
            dst_ref=slots.at[holder, part(k)],
            send_sem=cross_send.at[offset - 1, k],
            recv_sem=cross_recv.at[offset - 1, k],
            device_id=(target, samp),
            device_id_type=MESH,
        )

    def relay(offset, k, holder):
        return pltpu.make_async_remote_copy(
            src_ref=slots.at[holder, part(k)],
            dst_ref=slots.at[holder, part(k)],
            send_sem=relay_send.at[offset - 1, k],
            recv_sem=relay_recv.at[offset - 1, k],
            device_id=(sibling, samp),
            device_id_type=MESH,
        )

    def to_sibling(holder):
        return pltpu.make_async_remote_copy(
            src_ref=tier_ref,
            dst_ref=slots.at[holder],
            send_sem=sib_send,
            recv_sem=sib_recv,
            device_id=(sibling, samp),
            device_id_type=MESH,
        )

    for offset in range(1, chips):
        @pl.loop(0, chunks)
        def _(k):
            cross(offset, k, feat, far(offset)).start()
    to_sibling(feat).start()

    flat = table.reshape(n_feat * rows * 4, lanes)

    def widen(holder, k):
        @pl.loop(0, step // 64 if step % 64 == 0 else 1)
        def _(g):
            size = 64 if step % 64 == 0 else step
            start = pl.multiple_of(k * step + g * size, size)
            for j in range(pieces):
                values = slots[holder, pl.ds(start, size), j * lanes:(j + 1) * lanes]
                flat[pl.ds(4 * (holder * rows + start) + j, size, stride=4), :] = values.astype(jnp.float32)

    small_copies = [
        pltpu.make_async_copy(pair_any, pair_vmem, small_sems.at[0]),
        pltpu.make_async_copy(res_any, res_ref, small_sems.at[1]),
        pltpu.make_async_copy(pair_any, pair_smem, small_sems.at[2]),
    ]
    for copy in small_copies:
        copy.start()
    for copy in small_copies:
        copy.wait()

    weights[:, :lanes] = res_ref[...]
    weights[:, lanes:] = jnp.ones((samples, lanes), jnp.bfloat16)
    col_local = jnp.sum(res_ref[...].astype(jnp.float32), axis=0, keepdims=True)

    @pl.loop(0, pairs // lanes)
    def _(g):
        span = pl.ds(pl.multiple_of(g * lanes, lanes), lanes)
        op_wide[span, :] = jnp.broadcast_to(pair_vmem[g, 2:3, :], (lanes, lanes)).T

    own_copy.wait()

    @pl.loop(0, chunks)
    def _(k):
        widen(feat, k)

    to_sibling(sibling).wait_recv()

    @pl.loop(0, chunks)
    def _(k):
        widen(sibling, k)

    for offset in range(1, chips):
        mine = far(chips - offset)
        theirs = mine + 1 - 2 * core

        @pl.loop(0, chunks)
        def _(k):
            cross(offset, k, mine, feat).wait_recv()
            relay(offset, k, mine).start()
            widen(mine, k)

            @pl.when(k > 0)
            def _():
                relay(offset, k - 1, theirs).wait_recv()
                widen(theirs, k - 1)

        relay(offset, chunks - 1, theirs).wait_recv()
        widen(theirs, chunks - 1)

    lane_id = lax.broadcasted_iota(jnp.int32, (sub, lanes), 1)

    couples = owned // (2 * sub)
    count = half * couples
    lead = count * 5 // 8

    def unit(r):
        k = r - lead
        mixed = r < 2 * count - lead
        ours = jnp.where(r < lead, 0, jnp.where(mixed, lax.rem(k + 1, 2), 1))
        m = jnp.where(r < lead, r, jnp.where(mixed, k // 2 + lead * lax.rem(k, 2), r - count))
        t = m // couples
        h = lax.rem(m, couples)
        owner = lax.rem(high + 1 + t, half) * 2 + lax.rem(low + 1 + ours, 2)
        return ours, m, t, h, owner

    def base_of(r):
        _, _, _, h, owner = unit(r)
        return owner * owned + h * (2 * sub)

    def index_of(which, base, p):
        inside = 0 if sub % lanes == 0 else lax.rem(base, lanes)
        return pair_smem[base // lanes, which, inside + p]

    def fetch(base, p):
        return (
            [table[index_of(0, base, p + u)] for u in range(group)],
            [table[index_of(1, base, p + u)] for u in range(group)],
        )

    def stage(stages, p, fetched):
        for u in range(group):
            stages[0][4 * (p + u):4 * (p + u) + 4, :] = fetched[0][u]
            stages[1][4 * (p + u):4 * (p + u) + 4, :] = fetched[1][u]

    def build(stages, base, p):
        op = op_wide[pl.ds(pl.multiple_of(base + p, tall), tall), :]
        parts = []
        square = jnp.zeros((tall, lanes), jnp.float32)
        for j in range(pieces):
            a = stages[0][pl.ds(4 * p + j, tall, stride=4), :]
            b = stages[1][pl.ds(4 * p + j, tall, stride=4), :]
            plain = a + jnp.where(op == 1, -b, b)
            other = jnp.where(op == 2, a * b, a / (1.0 + jnp.abs(b)))
            built = jnp.where(op < 2, plain, other).astype(jnp.bfloat16)
            parts.append(built)
            wide = built.astype(jnp.float32)
            square += wide * wide
        return jnp.concatenate(parts, axis=1), jnp.sum(square, axis=1, keepdims=True)

    def advance(now, base, later, next_base, here):
        built, squares = [], []
        steps = sub // tall
        share = sub // 2 // steps
        fetched = fetch(next_base, 0)
        for i in range(steps):
            one, square = build(now, base, i * tall)
            built.append(one)
            squares.append(square)
            for p in range(i * share, (i + 1) * share, group):
                following = fetch(next_base, p + group)
                stage(later, p, fetched)
                fetched = following
        both = jnp.dot(
            jnp.concatenate(built, axis=0), weights[...], preferred_element_type=jnp.float32
        )
        for p in range(sub // 2, sub, group):
            following = fetch(next_base, p + group) if p + group < sub else None
            stage(later, p, fetched)
            fetched = following
        sums = both[:, lanes:]
        share_block[here, :] = both[:, :lanes] - sums * (col_local / samples)
        stats_wide[here, :] = jnp.where(lane_id == 0, sums, jnp.concatenate(squares, axis=0))

    even = (first_even, second_even)
    odd = (first_odd, second_odd)

    @pl.loop(0, sub // group)
    def _(g):
        base = base_of(0)
        firsts = [table[index_of(0, base, g * group + u)] for u in range(group)]
        seconds = [table[index_of(1, base, g * group + u)] for u in range(group)]
        for u in range(group):
            spot = pl.ds(pl.multiple_of((g * group + u) * 4, 4), 4)
            first_even[spot, :] = firsts[u]
            second_even[spot, :] = seconds[u]

    def rows_of(h):
        return pl.ds(pl.multiple_of(h * (2 * sub), 2 * sub), 2 * sub)

    def near_copy(m):
        t, here = m // couples, rows_of(lax.rem(m, couples))
        return pltpu.make_async_remote_copy(
            src_ref=near_out.at[t, here],
            dst_ref=near_in.at[t, here],
            send_sem=near_send.at[m],
            recv_sem=near_recv.at[m],
            device_id=(feat, partner),
            device_id_type=MESH,
        )

    def line_copy(m, source, target):
        t, h = m // couples, lax.rem(m, couples)
        return pltpu.make_async_remote_copy(
            src_ref=line_out.at[t, rows_of(h)],
            dst_ref=line_in.at[source, rows_of(h)],
            send_sem=line_send.at[m],
            recv_sem=line_recv.at[source * couples + h],
            device_id=(feat, target * 2 + low),
            device_id_type=MESH,
        )

    def stats_copy(owner, source):
        return pltpu.make_async_remote_copy(
            src_ref=send_stats.at[owner],
            dst_ref=recv_stats.at[source],
            send_sem=stats_send.at[owner],
            recv_sem=stats_recv.at[source],
            device_id=(feat, owner),
            device_id_type=MESH,
        )

    @pl.loop(0, 2 * count)
    def _(r):
        ours, m, t, h, owner = unit(r)
        base = owner * owned + h * (2 * sub)
        advance(even, base, odd, base + sub, pl.ds(0, sub))
        advance(odd, base + sub, even, base_of(r + 1), pl.ds(sub, sub))
        for q in range(2 * sub // lanes):
            flipped = stats_wide[q * lanes:(q + 1) * lanes, :].T
            span = pl.ds(pl.multiple_of(h * (2 * sub) + q * lanes, lanes), lanes)
            send_stats[owner, 0:2, span] = flipped[0:2, :]
        send_stats[owner, 2:3, 0:lanes] = col_local
        here = rows_of(h)

        @pl.when(ours == 0)
        def _():
            near_out[t, here, :] = share_block[...].astype(jnp.bfloat16)
            near_copy(m).start()

        @pl.when(ours == 1)
        def _():
            near_copy(m).wait_recv()
            total = share_block[...] + near_in[t, here, :].astype(jnp.float32)
            line_out[t, here, :] = total.astype(jnp.bfloat16)
            out_ref[here, :] = total

            @pl.when(t < half - 1)
            def _():
                line_copy(m, high, lax.rem(high + 1 + t, half)).start()

        @pl.when((h == couples - 1) & (r < 2 * count - 1))
        def _():
            stats_copy(owner, samp).start()

    recv_stats[samp] = send_stats[samp]

    @pl.loop(1, n_samp)
    def _(t):
        stats_copy(samp, lax.rem(samp + n_samp - t, n_samp)).wait_recv()

    first_sums = jnp.zeros((1, owned), jnp.float32)
    square_sums = jnp.zeros((1, owned), jnp.float32)
    for d in range(n_samp):
        first_sums += recv_stats[d, 0:1, :]
        square_sums += recv_stats[d, 1:2, :]
    means = first_sums / total_samples
    variance = square_sums / total_samples - means * means
    turned[n_samp:n_samp + 1, :] = lax.rsqrt(variance + epsilon) / math.sqrt(total_samples)
    for d in range(n_samp):
        turned[d:d + 1, :] = recv_stats[d, 0:1, :] / samples - means

    @pl.loop(0, owned // lanes)
    def _(q):
        span = pl.ds(pl.multiple_of(q * lanes, lanes), lanes)
        columns = turned[:, span].T
        total = out_ref[span, :]
        for d in range(n_samp):
            total += columns[:, d:d + 1] * recv_stats[d, 2:3, 0:lanes]
        out_ref[span, :] = total
        scale[span, :] = jnp.broadcast_to(columns[:, n_samp:n_samp + 1], (lanes, lanes))

    @pl.loop(0, (half - 1) * couples)
    def _(m):
        source = lax.rem(high + half - 1 - m // couples, half)
        here = rows_of(lax.rem(m, couples))
        line_copy(m, source, high).wait_recv()
        out_ref[here, :] += line_in[source, here, :].astype(jnp.float32)

    out_ref[...] *= scale[...]

    to_sibling(feat).wait_send()
    for offset in range(1, chips):
        @pl.loop(0, chunks)
        def _(k):
            cross(offset, k, feat, far(offset)).wait_send()
            relay(offset, k, far(chips - offset)).wait_send()

    @pl.loop(0, count)
    def _(m):
        near_copy(m).wait_send()

    @pl.loop(0, (half - 1) * couples)
    def _(m):
        line_copy(m, high, lax.rem(high + 1 + m // couples, half)).wait_send()

    @pl.loop(1, n_samp)
    def _(t):
        stats_copy(lax.rem(samp + t, n_samp), samp).wait_send()


def per_device(n_feat, n_samp, tier_one, residuals, pair_list):
    rows, samples = tier_one.shape
    pairs = pair_list.shape[1]
    chips = n_feat // 2
    owned = pairs // n_samp
    sub = min(owned // 2, 128)
    chunks = 16
    sizes = (n_feat, n_samp, rows, samples, pairs, chunks)
    dma = pltpu.SemaphoreType.DMA
    tiled = pair_list.reshape(3, pairs // lanes, lanes).transpose(1, 0, 2)
    return pl.pallas_call(
        functools.partial(kernel, sizes),
        out_shape=jax.ShapeDtypeStruct((owned, lanes), jnp.float32),
        in_specs=[
            pl.BlockSpec(memory_space=pl.ANY),
            pl.BlockSpec(memory_space=pl.ANY),
            pl.BlockSpec(memory_space=pl.ANY),
        ],
        out_specs=pl.BlockSpec(memory_space=pltpu.VMEM),
        scratch_shapes=[
            pltpu.VMEM((samples, lanes), jnp.bfloat16),
            pltpu.SMEM((pairs // lanes, 3, lanes), jnp.int32),
            pltpu.VMEM((pairs // lanes, 3, lanes), jnp.int32),
            pltpu.VMEM((n_feat, rows, samples), jnp.bfloat16),
            pltpu.VMEM((n_feat * rows, 4, lanes), jnp.float32),
            pltpu.VMEM((sub * 4, lanes), jnp.float32),
            pltpu.VMEM((sub * 4, lanes), jnp.float32),
            pltpu.VMEM((sub * 4, lanes), jnp.float32),
            pltpu.VMEM((sub * 4, lanes), jnp.float32),
            pltpu.VMEM((pairs, lanes), jnp.int32),
            pltpu.VMEM((samples, 2 * lanes), jnp.bfloat16),
            pltpu.VMEM((2 * sub, lanes), jnp.float32),
            pltpu.VMEM((2 * sub, lanes), jnp.float32),
            pltpu.VMEM((n_samp // 2, owned, lanes), jnp.bfloat16),
            pltpu.VMEM((n_samp // 2, owned, lanes), jnp.bfloat16),
            pltpu.VMEM((n_samp // 2, owned, lanes), jnp.bfloat16),
            pltpu.VMEM((n_samp // 2, owned, lanes), jnp.bfloat16),
            pltpu.VMEM((n_samp, 4, owned), jnp.float32),
            pltpu.VMEM((n_samp, 4, owned), jnp.float32),
            pltpu.VMEM((lanes, owned), jnp.float32),
            pltpu.VMEM((owned, lanes), jnp.float32),
            dma,
            dma((3,)),
            dma((max(chips - 1, 1), chunks)),
            dma((max(chips - 1, 1), chunks)),
            dma,
            dma,
            dma((max(chips - 1, 1), chunks)),
            dma((max(chips - 1, 1), chunks)),
            dma((n_samp // 2 * (owned // (2 * sub)),)),
            dma((n_samp // 2 * (owned // (2 * sub)),)),
            dma((n_samp // 2 * (owned // (2 * sub)),)),
            dma((n_samp // 2 * (owned // (2 * sub)),)),
            dma((n_samp,)),
            dma((n_samp,)),
        ],
        compiler_params=pltpu.CompilerParams(
            collective_id=0, has_side_effects=True, vmem_limit_bytes=56 * 2**20
        ),
    )(tier_one, residuals, tiled)


def solution(mesh):
    in_specs = (P("feat", "samp"), P("samp", None), P(None, "feat"))
    out_specs = P(("feat", "samp"), None)
    return jax.shard_map(
        functools.partial(per_device, mesh.shape["feat"], mesh.shape["samp"]),
        mesh=mesh, in_specs=in_specs, out_specs=out_specs, check_vma=False,
    )
```

```python
import functools
import math

import jax
import jax.numpy as jnp
from jax import lax
from jax.experimental import pallas as pl
from jax.experimental.pallas import tpu as pltpu
from jax.sharding import PartitionSpec as P

epsilon = 1e-05
MESH = pl.DeviceIdType.MESH
lanes = 128


def kernel(
    sizes, tier_ref, res_any, pair_any, out_ref,
    res_ref, pair_smem, pair_vmem, slots, table, first_even, second_even, first_odd, second_odd,
    op_wide, weights, share_block, stats_wide,
    near_out, near_in, line_out, line_in, send_stats, recv_stats, turned, scale,
    own_sem, small_sems, cross_send, cross_recv, sib_send, sib_recv, relay_send, relay_recv,
    near_send, near_recv, line_send, line_recv, stats_send, stats_recv,
):
    n_feat, n_samp, rows, samples, pairs, chunks = sizes
    chips = n_feat // 2
    pieces = samples // lanes
    owned = pairs // n_samp
    sub = min(owned // 2, 128)
    group, tall = 8, 16
    step = rows // chunks
    total_samples = samples * n_samp
    feat = lax.axis_index("feat")
    samp = lax.axis_index("samp")
    chip = feat // 2
    core = lax.rem(feat, 2)
    sibling = chip * 2 + 1 - core
    half = n_samp // 2
    high = samp // 2
    low = lax.rem(samp, 2)
    partner = high * 2 + 1 - low

    def far(offset):
        return lax.rem(chip + offset, chips) * 2 + core

    barrier = pltpu.get_barrier_semaphore()
    pl.semaphore_signal(barrier, inc=1, device_id=(sibling, samp), device_id_type=MESH)
    for offset in range(1, chips):
        pl.semaphore_signal(barrier, inc=1, device_id=(far(offset), samp), device_id_type=MESH)
    for offset in range(1, n_samp):
        pl.semaphore_signal(
            barrier, inc=1, device_id=(feat, lax.rem(samp + offset, n_samp)), device_id_type=MESH
        )
    own_copy = pltpu.make_async_copy(tier_ref, slots.at[feat], own_sem)
    own_copy.start()
    pl.semaphore_wait(barrier, 1 + (chips - 1) + (n_samp - 1))

    def part(index):
        return pl.ds(pl.multiple_of(index * step, step), step)

    def cross(offset, k, holder, target):
        return pltpu.make_async_remote_copy(
            src_ref=tier_ref.at[part(k)],
            dst_ref=slots.at[holder, part(k)],
            send_sem=cross_send.at[offset - 1, k],
            recv_sem=cross_recv.at[offset - 1, k],
            device_id=(target, samp),
            device_id_type=MESH,
        )

    def relay(offset, k, holder):
        return pltpu.make_async_remote_copy(
            src_ref=slots.at[holder, part(k)],
            dst_ref=slots.at[holder, part(k)],
            send_sem=relay_send.at[offset - 1, k],
            recv_sem=relay_recv.at[offset - 1, k],
            device_id=(sibling, samp),
            device_id_type=MESH,
        )

    def to_sibling(holder):
        return pltpu.make_async_remote_copy(
            src_ref=tier_ref,
            dst_ref=slots.at[holder],
            send_sem=sib_send,
            recv_sem=sib_recv,
            device_id=(sibling, samp),
            device_id_type=MESH,
        )

    for offset in range(1, chips):
        @pl.loop(0, chunks)
        def _(k):
            cross(offset, k, feat, far(offset)).start()
    to_sibling(feat).start()

    flat = table.reshape(n_feat * rows * 4, lanes)

    def widen(holder, k):
        @pl.loop(0, step // 64 if step % 64 == 0 else 1)
        def _(g):
            size = 64 if step % 64 == 0 else step
            start = pl.multiple_of(k * step + g * size, size)
            for j in range(pieces):
                values = slots[holder, pl.ds(start, size), j * lanes:(j + 1) * lanes]
                flat[pl.ds(4 * (holder * rows + start) + j, size, stride=4), :] = values.astype(jnp.float32)

    small_copies = [
        pltpu.make_async_copy(pair_any, pair_vmem, small_sems.at[0]),
        pltpu.make_async_copy(res_any, res_ref, small_sems.at[1]),
        pltpu.make_async_copy(pair_any, pair_smem, small_sems.at[2]),
    ]
    for copy in small_copies:
        copy.start()
    for copy in small_copies:
        copy.wait()

    weights[:, :lanes] = res_ref[...]
    weights[:, lanes:] = jnp.ones((samples, lanes), jnp.bfloat16)
    col_local = jnp.sum(res_ref[...].astype(jnp.float32), axis=0, keepdims=True)

    @pl.loop(0, pairs // lanes)
    def _(g):
        span = pl.ds(pl.multiple_of(g * lanes, lanes), lanes)
        op_wide[span, :] = jnp.broadcast_to(pair_vmem[g, 2:3, :], (lanes, lanes)).T

    own_copy.wait()

    @pl.loop(0, chunks)
    def _(k):
        widen(feat, k)

    to_sibling(sibling).wait_recv()

    @pl.loop(0, chunks)
    def _(k):
        widen(sibling, k)

    for offset in range(1, chips):
        mine = far(chips - offset)
        theirs = mine + 1 - 2 * core

        @pl.loop(0, chunks)
        def _(k):
            cross(offset, k, mine, feat).wait_recv()
            relay(offset, k, mine).start()
            widen(mine, k)

            @pl.when(k > 0)
            def _():
                relay(offset, k - 1, theirs).wait_recv()
                widen(theirs, k - 1)

        relay(offset, chunks - 1, theirs).wait_recv()
        widen(theirs, chunks - 1)

    lane_id = lax.broadcasted_iota(jnp.int32, (sub, lanes), 1)

    couples = owned // (2 * sub)
    count = half * couples
    lead = count * 5 // 8

    def unit(r):
        k = r - lead
        mixed = r < 2 * count - lead
        ours = jnp.where(r < lead, 0, jnp.where(mixed, lax.rem(k + 1, 2), 1))
        m = jnp.where(r < lead, r, jnp.where(mixed, k // 2 + lead * lax.rem(k, 2), r - count))
        t = m // couples
        h = lax.rem(m, couples)
        owner = lax.rem(high + 1 + t, half) * 2 + lax.rem(low + 1 + ours, 2)
        return ours, m, t, h, owner

    def base_of(r):
        _, _, _, h, owner = unit(r)
        return owner * owned + h * (2 * sub)

    def index_of(which, base, p):
        inside = 0 if sub % lanes == 0 else lax.rem(base, lanes)
        return pair_smem[base // lanes, which, inside + p]

    def fetch(base, p):
        return (
            [table[index_of(0, base, p + u)] for u in range(group)],
            [table[index_of(1, base, p + u)] for u in range(group)],
        )

    def stage(stages, p, fetched):
        for u in range(group):
            stages[0][pieces * (p + u):pieces * (p + u + 1), :] = fetched[0][u][:pieces]
            stages[1][pieces * (p + u):pieces * (p + u + 1), :] = fetched[1][u][:pieces]

    def build(stages, base, p):
        op = op_wide[pl.ds(pl.multiple_of(base + p, tall), tall), :]
        parts = []
        square = jnp.zeros((tall, lanes), jnp.float32)
        for j in range(pieces):
            a = stages[0][pl.ds(pieces * p + j, tall, stride=pieces), :]
            b = stages[1][pl.ds(pieces * p + j, tall, stride=pieces), :]
            plain = a + jnp.where(op == 1, -b, b)
            other = jnp.where(op == 2, a * b, a / (1.0 + jnp.abs(b)))
            built = jnp.where(op < 2, plain, other).astype(jnp.bfloat16)
            parts.append(built)
            wide = built.astype(jnp.float32)
            square += wide * wide
        return jnp.concatenate(parts, axis=1), jnp.sum(square, axis=1, keepdims=True)

    def advance(now, base, later, next_base, here):
        built, squares = [], []
        steps = sub // tall
        share = sub // 2 // steps
        fetched = fetch(next_base, 0)
        for i in range(steps):
            one, square = build(now, base, i * tall)
            built.append(one)
            squares.append(square)
            for p in range(i * share, (i + 1) * share, group):
                following = fetch(next_base, p + group)
                stage(later, p, fetched)
                fetched = following
        both = jnp.dot(
            jnp.concatenate(built, axis=0), weights[...], preferred_element_type=jnp.float32
        )
        for p in range(sub // 2, sub, group):
            following = fetch(next_base, p + group) if p + group < sub else None
            stage(later, p, fetched)
            fetched = following
        sums = both[:, lanes:]
        share_block[here, :] = both[:, :lanes] - sums * (col_local / samples)
        stats_wide[here, :] = jnp.where(lane_id == 0, sums, jnp.concatenate(squares, axis=0))

    even = (first_even, second_even)
    odd = (first_odd, second_odd)

    @pl.loop(0, sub // group)
    def _(g):
        base = base_of(0)
        firsts = [table[index_of(0, base, g * group + u)] for u in range(group)]
        seconds = [table[index_of(1, base, g * group + u)] for u in range(group)]
        for u in range(group):
            spot = pl.ds(pl.multiple_of(g * (group * pieces), 8) + pieces * u, pieces)
            first_even[spot, :] = firsts[u][:pieces]
            second_even[spot, :] = seconds[u][:pieces]

    def rows_of(h):
        return pl.ds(pl.multiple_of(h * (2 * sub), 2 * sub), 2 * sub)

    def near_copy(m):
        t, here = m // couples, rows_of(lax.rem(m, couples))
        return pltpu.make_async_remote_copy(
            src_ref=near_out.at[t, here],
            dst_ref=near_in.at[t, here],
            send_sem=near_send.at[m],
            recv_sem=near_recv.at[m],
            device_id=(feat, partner),
            device_id_type=MESH,
        )

    def line_copy(m, source, target):
        t, h = m // couples, lax.rem(m, couples)
        return pltpu.make_async_remote_copy(
            src_ref=line_out.at[t, rows_of(h)],
            dst_ref=line_in.at[source, rows_of(h)],
            send_sem=line_send.at[m],
            recv_sem=line_recv.at[source * couples + h],
            device_id=(feat, target * 2 + low),
            device_id_type=MESH,
        )

    def stats_copy(owner, source):
        return pltpu.make_async_remote_copy(
            src_ref=send_stats.at[owner],
            dst_ref=recv_stats.at[source],
            send_sem=stats_send.at[owner],
            recv_sem=stats_recv.at[source],
            device_id=(feat, owner),
            device_id_type=MESH,
        )

    @pl.loop(0, 2 * count)
    def _(r):
        ours, m, t, h, owner = unit(r)
        base = owner * owned + h * (2 * sub)
        advance(even, base, odd, base + sub, pl.ds(0, sub))
        advance(odd, base + sub, even, base_of(r + 1), pl.ds(sub, sub))
        for q in range(2 * sub // lanes):
            flipped = stats_wide[q * lanes:(q + 1) * lanes, :].T
            span = pl.ds(pl.multiple_of(h * (2 * sub) + q * lanes, lanes), lanes)
            send_stats[owner, 0:2, span] = flipped[0:2, :]
        send_stats[owner, 2:3, 0:lanes] = col_local
        here = rows_of(h)

        @pl.when(ours == 0)
        def _():
            near_out[t, here, :] = share_block[...].astype(jnp.bfloat16)
            near_copy(m).start()

        @pl.when(ours == 1)
        def _():
            near_copy(m).wait_recv()
            total = share_block[...] + near_in[t, here, :].astype(jnp.float32)
            line_out[t, here, :] = total.astype(jnp.bfloat16)
            out_ref[here, :] = total

            @pl.when(t < half - 1)
            def _():
                line_copy(m, high, lax.rem(high + 1 + t, half)).start()

        @pl.when((h == couples - 1) & (r < 2 * count - 1))
        def _():
            stats_copy(owner, samp).start()

    recv_stats[samp] = send_stats[samp]

    @pl.loop(1, n_samp)
    def _(t):
        stats_copy(samp, lax.rem(samp + n_samp - t, n_samp)).wait_recv()

    first_sums = jnp.zeros((1, owned), jnp.float32)
    square_sums = jnp.zeros((1, owned), jnp.float32)
    for d in range(n_samp):
        first_sums += recv_stats[d, 0:1, :]
        square_sums += recv_stats[d, 1:2, :]
    means = first_sums / total_samples
    variance = square_sums / total_samples - means * means
    turned[n_samp:n_samp + 1, :] = lax.rsqrt(variance + epsilon) / math.sqrt(total_samples)
    for d in range(n_samp):
        turned[d:d + 1, :] = recv_stats[d, 0:1, :] / samples - means

    @pl.loop(0, owned // lanes)
    def _(q):
        span = pl.ds(pl.multiple_of(q * lanes, lanes), lanes)
        columns = turned[:, span].T
        total = out_ref[span, :]
        for d in range(n_samp):
            total += columns[:, d:d + 1] * recv_stats[d, 2:3, 0:lanes]
        out_ref[span, :] = total
        scale[span, :] = jnp.broadcast_to(columns[:, n_samp:n_samp + 1], (lanes, lanes))

    @pl.loop(0, (half - 1) * couples)
    def _(m):
        source = lax.rem(high + half - 1 - m // couples, half)
        here = rows_of(lax.rem(m, couples))
        line_copy(m, source, high).wait_recv()
        out_ref[here, :] += line_in[source, here, :].astype(jnp.float32)

    out_ref[...] *= scale[...]

    to_sibling(feat).wait_send()
    for offset in range(1, chips):
        @pl.loop(0, chunks)
        def _(k):
            cross(offset, k, feat, far(offset)).wait_send()
            relay(offset, k, far(chips - offset)).wait_send()

    @pl.loop(0, count)
    def _(m):
        near_copy(m).wait_send()

    @pl.loop(0, (half - 1) * couples)
    def _(m):
        line_copy(m, high, lax.rem(high + 1 + m // couples, half)).wait_send()

    @pl.loop(1, n_samp)
    def _(t):
        stats_copy(lax.rem(samp + t, n_samp), samp).wait_send()


def per_device(n_feat, n_samp, tier_one, residuals, pair_list):
    rows, samples = tier_one.shape
    pairs = pair_list.shape[1]
    chips = n_feat // 2
    owned = pairs // n_samp
    sub = min(owned // 2, 128)
    chunks = 16
    sizes = (n_feat, n_samp, rows, samples, pairs, chunks)
    dma = pltpu.SemaphoreType.DMA
    tiled = pair_list.reshape(3, pairs // lanes, lanes).transpose(1, 0, 2)
    return pl.pallas_call(
        functools.partial(kernel, sizes),
        out_shape=jax.ShapeDtypeStruct((owned, lanes), jnp.float32),
        in_specs=[
            pl.BlockSpec(memory_space=pl.ANY),
            pl.BlockSpec(memory_space=pl.ANY),
            pl.BlockSpec(memory_space=pl.ANY),
        ],
        out_specs=pl.BlockSpec(memory_space=pltpu.VMEM),
        scratch_shapes=[
            pltpu.VMEM((samples, lanes), jnp.bfloat16),
            pltpu.SMEM((pairs // lanes, 3, lanes), jnp.int32),
            pltpu.VMEM((pairs // lanes, 3, lanes), jnp.int32),
            pltpu.VMEM((n_feat, rows, samples), jnp.bfloat16),
            pltpu.VMEM((n_feat * rows, 4, lanes), jnp.float32),
            pltpu.VMEM((sub * (samples // lanes), lanes), jnp.float32),
            pltpu.VMEM((sub * (samples // lanes), lanes), jnp.float32),
            pltpu.VMEM((sub * (samples // lanes), lanes), jnp.float32),
            pltpu.VMEM((sub * (samples // lanes), lanes), jnp.float32),
            pltpu.VMEM((pairs, lanes), jnp.int32),
            pltpu.VMEM((samples, 2 * lanes), jnp.bfloat16),
            pltpu.VMEM((2 * sub, lanes), jnp.float32),
            pltpu.VMEM((2 * sub, lanes), jnp.float32),
            pltpu.VMEM((n_samp // 2, owned, lanes), jnp.bfloat16),
            pltpu.VMEM((n_samp // 2, owned, lanes), jnp.bfloat16),
            pltpu.VMEM((n_samp // 2, owned, lanes), jnp.bfloat16),
            pltpu.VMEM((n_samp // 2, owned, lanes), jnp.bfloat16),
            pltpu.VMEM((n_samp, 4, owned), jnp.float32),
            pltpu.VMEM((n_samp, 4, owned), jnp.float32),
            pltpu.VMEM((lanes, owned), jnp.float32),
            pltpu.VMEM((owned, lanes), jnp.float32),
            dma,
            dma((3,)),
            dma((max(chips - 1, 1), chunks)),
            dma((max(chips - 1, 1), chunks)),
            dma,
            dma,
            dma((max(chips - 1, 1), chunks)),
            dma((max(chips - 1, 1), chunks)),
            dma((n_samp // 2 * (owned // (2 * sub)),)),
            dma((n_samp // 2 * (owned // (2 * sub)),)),
            dma((n_samp // 2 * (owned // (2 * sub)),)),
            dma((n_samp // 2 * (owned // (2 * sub)),)),
            dma((n_samp,)),
            dma((n_samp,)),
        ],
        compiler_params=pltpu.CompilerParams(
            collective_id=0, has_side_effects=True, vmem_limit_bytes=56 * 2**20
        ),
    )(tier_one, residuals, tiled)


def solution(mesh):
    in_specs = (P("feat", "samp"), P("samp", None), P(None, "feat"))
    out_specs = P(("feat", "samp"), None)
    return jax.shard_map(
        functools.partial(per_device, mesh.shape["feat"], mesh.shape["samp"]),
        mesh=mesh, in_specs=in_specs, out_specs=out_specs, check_vma=False,
    )
```

```python
import functools
import math

import jax
import jax.numpy as jnp
from jax import lax
from jax.experimental import pallas as pl
from jax.experimental.pallas import tpu as pltpu
from jax.sharding import PartitionSpec as P

epsilon = 1e-05
MESH = pl.DeviceIdType.MESH
lanes = 128


def kernel(
    sizes, tier_ref, res_any, pair_any, out_ref,
    res_ref, pair_smem, pair_vmem, slots, table, first_even, second_even, first_odd, second_odd,
    op_wide, weights, share_block, stats_wide,
    near_out, near_in, line_out, line_in, send_stats, recv_stats, turned, scale,
    own_sem, small_sems, cross_send, cross_recv, sib_send, sib_recv, relay_send, relay_recv,
    near_send, near_recv, line_send, line_recv, stats_send, stats_recv,
):
    n_feat, n_samp, rows, samples, pairs, chunks = sizes
    chips = n_feat // 2
    pieces = samples // lanes
    owned = pairs // n_samp
    sub = min(owned // 2, 128)
    group, tall = 8, 16
    step = rows // chunks
    total_samples = samples * n_samp
    feat = lax.axis_index("feat")
    samp = lax.axis_index("samp")
    chip = feat // 2
    core = lax.rem(feat, 2)
    sibling = chip * 2 + 1 - core
    half = n_samp // 2
    high = samp // 2
    low = lax.rem(samp, 2)
    partner = high * 2 + 1 - low

    def far(offset):
        return lax.rem(chip + offset, chips) * 2 + core

    barrier = pltpu.get_barrier_semaphore()
    pl.semaphore_signal(barrier, inc=1, device_id=(sibling, samp), device_id_type=MESH)
    for offset in range(1, chips):
        pl.semaphore_signal(barrier, inc=1, device_id=(far(offset), samp), device_id_type=MESH)
    for offset in range(1, n_samp):
        pl.semaphore_signal(
            barrier, inc=1, device_id=(feat, lax.rem(samp + offset, n_samp)), device_id_type=MESH
        )
    own_copy = pltpu.make_async_copy(tier_ref, slots.at[feat], own_sem)
    own_copy.start()
    pl.semaphore_wait(barrier, 1 + (chips - 1) + (n_samp - 1))

    def part(index):
        return pl.ds(pl.multiple_of(index * step, step), step)

    def cross(offset, k, holder, target):
        return pltpu.make_async_remote_copy(
            src_ref=tier_ref.at[part(k)],
            dst_ref=slots.at[holder, part(k)],
            send_sem=cross_send.at[offset - 1, k],
            recv_sem=cross_recv.at[offset - 1, k],
            device_id=(target, samp),
            device_id_type=MESH,
        )

    def relay(offset, k, holder):
        return pltpu.make_async_remote_copy(
            src_ref=slots.at[holder, part(k)],
            dst_ref=slots.at[holder, part(k)],
            send_sem=relay_send.at[offset - 1, k],
            recv_sem=relay_recv.at[offset - 1, k],
            device_id=(sibling, samp),
            device_id_type=MESH,
        )

    def to_sibling(holder):
        return pltpu.make_async_remote_copy(
            src_ref=tier_ref,
            dst_ref=slots.at[holder],
            send_sem=sib_send,
            recv_sem=sib_recv,
            device_id=(sibling, samp),
            device_id_type=MESH,
        )

    for offset in range(1, chips):
        @pl.loop(0, chunks)
        def _(k):
            cross(offset, k, feat, far(offset)).start()
    to_sibling(feat).start()

    flat = table.reshape(n_feat * rows * 4, lanes)

    def widen(holder, k):
        @pl.loop(0, step // 64 if step % 64 == 0 else 1)
        def _(g):
            size = 64 if step % 64 == 0 else step
            start = pl.multiple_of(k * step + g * size, size)
            for j in range(pieces):
                values = slots[holder, pl.ds(start, size), j * lanes:(j + 1) * lanes]
                flat[pl.ds(4 * (holder * rows + start) + j, size, stride=4), :] = values.astype(jnp.float32)

    small_copies = [
        pltpu.make_async_copy(pair_any, pair_vmem, small_sems.at[0]),
        pltpu.make_async_copy(res_any, res_ref, small_sems.at[1]),
        pltpu.make_async_copy(pair_any, pair_smem, small_sems.at[2]),
    ]
    for copy in small_copies:
        copy.start()
    for copy in small_copies:
        copy.wait()

    weights[:, :lanes] = res_ref[...]
    weights[:, lanes:] = jnp.ones((samples, lanes), jnp.bfloat16)
    col_local = jnp.sum(res_ref[...].astype(jnp.float32), axis=0, keepdims=True)

    @pl.loop(0, pairs // lanes)
    def _(g):
        span = pl.ds(pl.multiple_of(g * lanes, lanes), lanes)
        op_wide[span, :] = jnp.broadcast_to(pair_vmem[g, 2:3, :], (lanes, lanes)).T

    own_copy.wait()

    @pl.loop(0, chunks)
    def _(k):
        widen(feat, k)

    to_sibling(sibling).wait_recv()

    @pl.loop(0, chunks)
    def _(k):
        widen(sibling, k)

    for offset in range(1, chips):
        mine = far(chips - offset)
        theirs = mine + 1 - 2 * core

        @pl.loop(0, chunks)
        def _(k):
            cross(offset, k, mine, feat).wait_recv()
            relay(offset, k, mine).start()
            widen(mine, k)

            @pl.when(k > 0)
            def _():
                relay(offset, k - 1, theirs).wait_recv()
                widen(theirs, k - 1)

        relay(offset, chunks - 1, theirs).wait_recv()
        widen(theirs, chunks - 1)

    lane_id = lax.broadcasted_iota(jnp.int32, (sub, lanes), 1)

    couples = owned // (2 * sub)
    count = half * couples
    lead = count * 3 // 8

    def unit(r):
        k = r - lead
        mixed = r < 2 * count - lead
        ours = jnp.where(r < lead, 0, jnp.where(mixed, lax.rem(k + 1, 2), 1))
        m = jnp.where(r < lead, r, jnp.where(mixed, k // 2 + lead * lax.rem(k, 2), r - count))
        t = m // couples
        h = lax.rem(m, couples)
        owner = lax.rem(high + 1 + t, half) * 2 + lax.rem(low + 1 + ours, 2)
        return ours, m, t, h, owner

    def base_of(r):
        _, _, _, h, owner = unit(r)
        return owner * owned + h * (2 * sub)

    def index_of(which, base, p):
        inside = 0 if sub % lanes == 0 else lax.rem(base, lanes)
        return pair_smem[base // lanes, which, inside + p]

    def fetch(base, p):
        return (
            [table[index_of(0, base, p + u)] for u in range(group)],
            [table[index_of(1, base, p + u)] for u in range(group)],
        )

    def stage(stages, p, fetched):
        for u in range(group):
            stages[0][4 * (p + u):4 * (p + u) + 4, :] = fetched[0][u]
            stages[1][4 * (p + u):4 * (p + u) + 4, :] = fetched[1][u]

    def build(stages, base, p):
        op = op_wide[pl.ds(pl.multiple_of(base + p, tall), tall), :]
        parts = []
        square = jnp.zeros((tall, lanes), jnp.float32)
        for j in range(pieces):
            a = stages[0][pl.ds(4 * p + j, tall, stride=4), :]
            b = stages[1][pl.ds(4 * p + j, tall, stride=4), :]
            plain = a + jnp.where(op == 1, -b, b)
            other = jnp.where(op == 2, a * b, a / (1.0 + jnp.abs(b)))
            built = jnp.where(op < 2, plain, other).astype(jnp.bfloat16)
            parts.append(built)
            wide = built.astype(jnp.float32)
            square += wide * wide
        return jnp.concatenate(parts, axis=1), jnp.sum(square, axis=1, keepdims=True)

    def advance(now, base, later, next_base, here):
        built, squares = [], []
        steps = sub // tall
        share = sub // 2 // steps
        fetched = fetch(next_base, 0)
        for i in range(steps):
            one, square = build(now, base, i * tall)
            built.append(one)
            squares.append(square)
            for p in range(i * share, (i + 1) * share, group):
                following = fetch(next_base, p + group)
                stage(later, p, fetched)
                fetched = following
        both = jnp.dot(
            jnp.concatenate(built, axis=0), weights[...], preferred_element_type=jnp.float32
        )
        for p in range(sub // 2, sub, group):
            following = fetch(next_base, p + group) if p + group < sub else None
            stage(later, p, fetched)
            fetched = following
        sums = both[:, lanes:]
        share_block[here, :] = both[:, :lanes] - sums * (col_local / samples)
        stats_wide[here, :] = jnp.where(lane_id == 0, sums, jnp.concatenate(squares, axis=0))

    even = (first_even, second_even)
    odd = (first_odd, second_odd)

    @pl.loop(0, sub // group)
    def _(g):
        base = base_of(0)
        firsts = [table[index_of(0, base, g * group + u)] for u in range(group)]
        seconds = [table[index_of(1, base, g * group + u)] for u in range(group)]
        for u in range(group):
            spot = pl.ds(pl.multiple_of((g * group + u) * 4, 4), 4)
            first_even[spot, :] = firsts[u]
            second_even[spot, :] = seconds[u]

    def rows_of(h):
        return pl.ds(pl.multiple_of(h * (2 * sub), 2 * sub), 2 * sub)

    def near_copy(m):
        t, here = m // couples, rows_of(lax.rem(m, couples))
        return pltpu.make_async_remote_copy(
            src_ref=near_out.at[t, here],
            dst_ref=near_in.at[t, here],
            send_sem=near_send.at[m],
            recv_sem=near_recv.at[m],
            device_id=(feat, partner),
            device_id_type=MESH,
        )

    def line_copy(m, source, target):
        t, h = m // couples, lax.rem(m, couples)
        return pltpu.make_async_remote_copy(
            src_ref=line_out.at[t, rows_of(h)],
            dst_ref=line_in.at[source, rows_of(h)],
            send_sem=line_send.at[m],
            recv_sem=line_recv.at[source * couples + h],
            device_id=(feat, target * 2 + low),
            device_id_type=MESH,
        )

    def stats_copy(owner, source):
        return pltpu.make_async_remote_copy(
            src_ref=send_stats.at[owner],
            dst_ref=recv_stats.at[source],
            send_sem=stats_send.at[owner],
            recv_sem=stats_recv.at[source],
            device_id=(feat, owner),
            device_id_type=MESH,
        )

    @pl.loop(0, 2 * count)
    def _(r):
        ours, m, t, h, owner = unit(r)
        base = owner * owned + h * (2 * sub)
        advance(even, base, odd, base + sub, pl.ds(0, sub))
        advance(odd, base + sub, even, base_of(r + 1), pl.ds(sub, sub))
        for q in range(2 * sub // lanes):
            flipped = stats_wide[q * lanes:(q + 1) * lanes, :].T
            span = pl.ds(pl.multiple_of(h * (2 * sub) + q * lanes, lanes), lanes)
            send_stats[owner, 0:2, span] = flipped[0:2, :]
        send_stats[owner, 2:3, 0:lanes] = col_local
        here = rows_of(h)

        @pl.when(ours == 0)
        def _():
            near_out[t, here, :] = share_block[...].astype(jnp.bfloat16)
            near_copy(m).start()

        @pl.when(ours == 1)
        def _():
            near_copy(m).wait_recv()
            total = share_block[...] + near_in[t, here, :].astype(jnp.float32)
            line_out[t, here, :] = total.astype(jnp.bfloat16)
            out_ref[here, :] = total

            @pl.when(t < half - 1)
            def _():
                line_copy(m, high, lax.rem(high + 1 + t, half)).start()

        @pl.when((h == couples - 1) & (r < 2 * count - 1))
        def _():
            stats_copy(owner, samp).start()

    recv_stats[samp] = send_stats[samp]

    @pl.loop(1, n_samp)
    def _(t):
        stats_copy(samp, lax.rem(samp + n_samp - t, n_samp)).wait_recv()

    first_sums = jnp.zeros((1, owned), jnp.float32)
    square_sums = jnp.zeros((1, owned), jnp.float32)
    for d in range(n_samp):
        first_sums += recv_stats[d, 0:1, :]
        square_sums += recv_stats[d, 1:2, :]
    means = first_sums / total_samples
    variance = square_sums / total_samples - means * means
    turned[n_samp:n_samp + 1, :] = lax.rsqrt(variance + epsilon) / math.sqrt(total_samples)
    for d in range(n_samp):
        turned[d:d + 1, :] = recv_stats[d, 0:1, :] / samples - means

    @pl.loop(0, owned // lanes)
    def _(q):
        span = pl.ds(pl.multiple_of(q * lanes, lanes), lanes)
        columns = turned[:, span].T
        total = out_ref[span, :]
        for d in range(n_samp):
            total += columns[:, d:d + 1] * recv_stats[d, 2:3, 0:lanes]
        out_ref[span, :] = total
        scale[span, :] = jnp.broadcast_to(columns[:, n_samp:n_samp + 1], (lanes, lanes))

    @pl.loop(0, (half - 1) * couples)
    def _(m):
        source = lax.rem(high + half - 1 - m // couples, half)
        here = rows_of(lax.rem(m, couples))
        line_copy(m, source, high).wait_recv()
        out_ref[here, :] += line_in[source, here, :].astype(jnp.float32)

    out_ref[...] *= scale[...]

    to_sibling(feat).wait_send()
    for offset in range(1, chips):
        @pl.loop(0, chunks)
        def _(k):
            cross(offset, k, feat, far(offset)).wait_send()
            relay(offset, k, far(chips - offset)).wait_send()

    @pl.loop(0, count)
    def _(m):
        near_copy(m).wait_send()

    @pl.loop(0, (half - 1) * couples)
    def _(m):
        line_copy(m, high, lax.rem(high + 1 + m // couples, half)).wait_send()

    @pl.loop(1, n_samp)
    def _(t):
        stats_copy(lax.rem(samp + t, n_samp), samp).wait_send()


def per_device(n_feat, n_samp, tier_one, residuals, pair_list):
    rows, samples = tier_one.shape
    pairs = pair_list.shape[1]
    chips = n_feat // 2
    owned = pairs // n_samp
    sub = min(owned // 2, 128)
    chunks = 16
    sizes = (n_feat, n_samp, rows, samples, pairs, chunks)
    dma = pltpu.SemaphoreType.DMA
    tiled = pair_list.reshape(3, pairs // lanes, lanes).transpose(1, 0, 2)
    return pl.pallas_call(
        functools.partial(kernel, sizes),
        out_shape=jax.ShapeDtypeStruct((owned, lanes), jnp.float32),
        in_specs=[
            pl.BlockSpec(memory_space=pl.ANY),
            pl.BlockSpec(memory_space=pl.ANY),
            pl.BlockSpec(memory_space=pl.ANY),
        ],
        out_specs=pl.BlockSpec(memory_space=pltpu.VMEM),
        scratch_shapes=[
            pltpu.VMEM((samples, lanes), jnp.bfloat16),
            pltpu.SMEM((pairs // lanes, 3, lanes), jnp.int32),
            pltpu.VMEM((pairs // lanes, 3, lanes), jnp.int32),
            pltpu.VMEM((n_feat, rows, samples), jnp.bfloat16),
            pltpu.VMEM((n_feat * rows, 4, lanes), jnp.float32),
            pltpu.VMEM((sub * 4, lanes), jnp.float32),
            pltpu.VMEM((sub * 4, lanes), jnp.float32),
            pltpu.VMEM((sub * 4, lanes), jnp.float32),
            pltpu.VMEM((sub * 4, lanes), jnp.float32),
            pltpu.VMEM((pairs, lanes), jnp.int32),
            pltpu.VMEM((samples, 2 * lanes), jnp.bfloat16),
            pltpu.VMEM((2 * sub, lanes), jnp.float32),
            pltpu.VMEM((2 * sub, lanes), jnp.float32),
            pltpu.VMEM((n_samp // 2, owned, lanes), jnp.bfloat16),
            pltpu.VMEM((n_samp // 2, owned, lanes), jnp.bfloat16),
            pltpu.VMEM((n_samp // 2, owned, lanes), jnp.bfloat16),
            pltpu.VMEM((n_samp // 2, owned, lanes), jnp.bfloat16),
            pltpu.VMEM((n_samp, 4, owned), jnp.float32),
            pltpu.VMEM((n_samp, 4, owned), jnp.float32),
            pltpu.VMEM((lanes, owned), jnp.float32),
            pltpu.VMEM((owned, lanes), jnp.float32),
            dma,
            dma((3,)),
            dma((max(chips - 1, 1), chunks)),
            dma((max(chips - 1, 1), chunks)),
            dma,
            dma,
            dma((max(chips - 1, 1), chunks)),
            dma((max(chips - 1, 1), chunks)),
            dma((n_samp // 2 * (owned // (2 * sub)),)),
            dma((n_samp // 2 * (owned // (2 * sub)),)),
            dma((n_samp // 2 * (owned // (2 * sub)),)),
            dma((n_samp // 2 * (owned // (2 * sub)),)),
            dma((n_samp,)),
            dma((n_samp,)),
        ],
        compiler_params=pltpu.CompilerParams(
            collective_id=0, has_side_effects=True, vmem_limit_bytes=56 * 2**20
        ),
    )(tier_one, residuals, tiled)


def solution(mesh):
    in_specs = (P("feat", "samp"), P("samp", None), P(None, "feat"))
    out_specs = P(("feat", "samp"), None)
    return jax.shard_map(
        functools.partial(per_device, mesh.shape["feat"], mesh.shape["samp"]),
        mesh=mesh, in_specs=in_specs, out_specs=out_specs, check_vma=False,
    )
```
